32 devices in a mesh: row: 8 (over y, x, core), col: 4 (over z).
Axes of the slice: x: 2, y: 2, z: 4, core: 2. Of those that a mesh axis runs over, the one named last changes fastest.
Arguments:
- item_features: bfloat16 [16384, 256], P(('row', 'col')), may hold values from -6 to 6
- self_weight: bfloat16 [256, 256], replicated, may hold values from -0.375 to 0.375
- neighbor_weight: bfloat16 [256, 256], replicated, may hold values from -0.375 to 0.375
- layer_bias: float32 [256], replicated, may hold values from -3 to 3
- norm_gain: float32 [256], replicated, may hold values from 0.5 to 1.5
- blocks: bfloat16 [8, 4, 256, 128, 128], P('row', 'col'), may hold values from 0 to 0.0625
- block_rows: int32 [8, 4, 256], P('row', 'col'), may hold values from 0 to 15, as said below
- block_cols: int32 [8, 4, 256], P('row', 'col'), may hold values from 0 to 31, as said below
- counts: int32 [8, 4], P('row', 'col'), may hold values from 1 to 256, as said below
- queries: bfloat16 [512, 256], P(('row', 'col')), may hold values from -6 to 6
- candidates: int32 [512, 64], P(('row', 'col')), may hold values from 0 to 16383, as said below
- positions: int32 [512, 64], P(('row', 'col')), may hold values from 0 to 63, each once within a row
- position_table: float32 [64, 128], replicated, may hold values from -6 to 6
- tower_weight: float32 [128], replicated, may hold values from -0.5 to 0.5
- score_cotangent: bfloat16 [512, 64], P(('row', 'col')), may hold values from -6 to 6
Outputs:
- hidden: bfloat16 [16384, 256], P(('row', 'col'))
- scores: float32 [512, 64], P(('row', 'col'))
- item_grads: float32 [16384, 256], P(('row', 'col'))
The draws below stay inside these ranges and needn't reach their ends.
Inputs may be any that keep to these rules, and one draw needn't show every extreme that they name: Slots s >= counts[r, c] are not part of A. In every draw all devices of some row have 256 live slots. `block_rows`: the live slots of one device name distinct pairs of block row and block column. `block_cols`: the live slots of one device name distinct pairs of block row and block column. The candidates of requests of piece p (rows p * 16 to (p + 1) * 16 - 1) are items of column set p % 4; an item may appear several times.
All inputs are finite; a program needn't handle non-finite values.
Results may differ from the reference program's by a relative error of at most 0.04.
Values may be sent and summed in bfloat16 or wider, within the bound.
A program may use at most 128 MiB of HBM per device.

```python
import jax
import jax.numpy as jnp
from jax import lax

D = 256
POS_WIDTH = 128
BLK = 128
CANDS = 64
ITEMS_DEV = 512
BLOCKS_DEV = 256
REQ_DEV = 16
ITEMS = 16384
REQS = 512
N_ROW = 8
N_COL = 4


def layout_draw(key):
    row_blocks = N_COL * ITEMS_DEV // BLK
    col_blocks = N_ROW * ITEMS_DEV // BLK
    position_total = row_blocks * col_blocks
    base_key = jax.random.fold_in(key, 11)
    busy_key, spread_key, place_key = jax.random.split(base_key, 3)
    busy_row = jax.random.randint(busy_key, (), 0, N_ROW)
    spread = jax.random.randint(spread_key, (N_ROW, N_COL), max(BLOCKS_DEV // 8, 1), BLOCKS_DEV // 2 + 1)
    counts = jnp.where(jnp.arange(N_ROW)[:, None] == busy_row, BLOCKS_DEV, spread).astype(jnp.int32)
    device_keys = jax.random.split(place_key, N_ROW * N_COL)

    def one_device(subkey, device_count):
        shuffled = jax.random.permutation(subkey, position_total)[:BLOCKS_DEV]
        slot_index = jnp.arange(BLOCKS_DEV)
        ordered = jnp.sort(jnp.where(slot_index < device_count, shuffled, position_total + shuffled))
        return ordered % position_total
    placed = jax.vmap(one_device)(device_keys, counts.reshape(-1)).reshape(N_ROW, N_COL, BLOCKS_DEV)
    return (counts, (placed // col_blocks).astype(jnp.int32), (placed % col_blocks).astype(jnp.int32))


def draw_counts(key, part):
    return layout_draw(key)[0]


def draw_block_rows(key, part):
    return layout_draw(key)[1]


def draw_block_cols(key, part):
    return layout_draw(key)[2]


def draw_candidates(key, part):
    subkey = jax.random.fold_in(key, 23)
    device_total = N_ROW * N_COL
    local_rows = jax.random.randint(subkey, (device_total, REQ_DEV, CANDS), 0, N_ROW * ITEMS_DEV)
    column = (jnp.arange(device_total) % N_COL)[:, None, None]
    owner_row = local_rows // ITEMS_DEV
    item_ids = (owner_row * N_COL + column) * ITEMS_DEV + local_rows % ITEMS_DEV
    item_ids = item_ids.reshape(REQS, CANDS)
    item_ids = item_ids.at[0, 0].set(0)
    item_ids = item_ids.at[REQS - 1, 0].set(ITEMS - 1)
    return item_ids.astype(jnp.int32)


def levels(own_key, shape, shards, low, top_value):
    gain = 1.0
    for position, shards_of in shards:
        heights = jax.random.uniform(jax.random.fold_in(jax.random.fold_in(own_key, 6), position), (shards_of,), jnp.float32, low / len(shards), top_value / len(shards))
        gain = gain * jnp.repeat(jnp.exp(heights), shape[position] // shards_of).reshape((-1,) + (1,) * (len(shape) - 1 - position))
    return gain


def bell_draw(own_key, dims, scale, bound, pieces=(), kind=jnp.bfloat16):
    array = jax.random.normal(own_key, dims, jnp.float32) * scale
    if len(pieces) > 0:
        array = levels(own_key, dims, pieces, -0.22, 0.18) * array
    return jnp.clip(array, min=-bound, max=bound).astype(kind)


def setup_inputs(seed: int = 0) -> dict:
    arg_keys = jax.random.split(jax.random.key(seed), 16)
    return {
        "item_features": bell_draw(arg_keys[0], (ITEMS, D), 1.0, 6.0, ((0, 32),)),
        "self_weight": bell_draw(arg_keys[1], (D, D), D ** -0.5, 0.375),
        "neighbor_weight": bell_draw(arg_keys[2], (D, D), D ** -0.5, 0.375),
        "layer_bias": bell_draw(arg_keys[3], (D,), 0.5, 3.0, (), jnp.float32),
        "norm_gain": jnp.clip(1.0 + 0.1 * jax.random.normal(arg_keys[4], (D,), jnp.float32), 0.5, 1.5),
        "blocks": jnp.clip(0.0625 * jax.random.uniform(arg_keys[5], (N_ROW, N_COL, BLOCKS_DEV, BLK, BLK), jnp.float32) ** levels(arg_keys[5], (N_ROW, N_COL, BLOCKS_DEV, BLK, BLK), ((0, 8), (1, 4)), -0.2, 0.2), 0.0, 0.0625).astype(jnp.bfloat16),
        "block_rows": draw_block_rows(jax.random.fold_in(arg_keys[15], 71), 0),
        "block_cols": draw_block_cols(jax.random.fold_in(arg_keys[15], 71), 0),
        "counts": draw_counts(jax.random.fold_in(arg_keys[15], 71), 0),
        "queries": bell_draw(arg_keys[9], (REQS, D), 1.0, 6.0, ((0, 32),)),
        "candidates": draw_candidates(jax.random.fold_in(arg_keys[15], 71), 0),
        "positions": jax.vmap(lambda own: jax.random.permutation(own, CANDS))(jax.random.split(arg_keys[11], REQS)).reshape((REQS, CANDS)).astype(jnp.int32),
        "position_table": bell_draw(arg_keys[12], (CANDS, POS_WIDTH), 1.0, 6.0, (), jnp.float32),
        "tower_weight": bell_draw(arg_keys[13], (POS_WIDTH,), POS_WIDTH ** -0.5, 0.5, (), jnp.float32),
        "score_cotangent": bell_draw(arg_keys[14], (REQS, CANDS), 1.0, 6.0, ((0, 32),)),
    }


norm_eps = 1e-05

def normalize(preact, norm_gain):
    active = jax.nn.silu(preact)
    return norm_gain * active * lax.rsqrt(lax.optimization_barrier(jnp.mean(active * active, axis=-1, keepdims=True)) + norm_eps)

def round_part(value):
    return lax.optimization_barrier(value.astype(jnp.bfloat16)).astype(jnp.float32)

def reference(item_features, self_weight, neighbor_weight, layer_bias, norm_gain, blocks, block_rows, block_cols, counts, queries, candidates, positions, position_table, tower_weight, score_cotangent):
    row_blocks = N_COL * ITEMS_DEV // BLK
    col_blocks = N_ROW * ITEMS_DEV // BLK
    item_grid = item_features.reshape(N_ROW, N_COL, ITEMS_DEV, D)
    slot_index = jnp.arange(BLOCKS_DEV)

    def forward_row(row_index):

        def add_column(col_index, summed):
            source = lax.dynamic_index_in_dim(item_grid, col_index, 1, False).reshape(col_blocks, BLK, D)
            tile_set = blocks[row_index, col_index].astype(jnp.float32)
            is_live = (slot_index < counts[row_index, col_index]).astype(jnp.float32)
            gathered = source[block_cols[row_index, col_index]].astype(jnp.float32)
            product = jnp.einsum('nij,njd->nid', tile_set, gathered) * is_live[:, None, None]
            return summed + round_part(jax.ops.segment_sum(product, block_rows[row_index, col_index], row_blocks))
        return lax.fori_loop(0, N_COL, add_column, jnp.zeros((row_blocks, BLK, D), jnp.float32))
    aggregate = lax.map(forward_row, jnp.arange(N_ROW)).reshape(ITEMS, D)
    preact = jnp.dot(item_features, self_weight, preferred_element_type=jnp.float32)
    preact = preact + jnp.dot(aggregate.astype(jnp.bfloat16), neighbor_weight, preferred_element_type=jnp.float32) + layer_bias
    normed, pullback = jax.vjp(lambda value: normalize(value, norm_gain), preact)
    hidden = normed.astype(jnp.bfloat16)
    score_scale = D ** (-0.5)
    tower_values = lax.optimization_barrier(jnp.sum(jax.nn.relu(position_table) * tower_weight, axis=-1))
    device_total = N_ROW * N_COL
    cand_dev = candidates.reshape(device_total, REQ_DEV, CANDS)
    query_dev = queries.reshape(device_total, REQ_DEV, D)
    cot_dev = score_cotangent.reshape(device_total, REQ_DEV, CANDS)

    def score_device(pair):
        ids, query_rows = pair
        picked = hidden[ids].astype(jnp.float32)
        return lax.optimization_barrier(jnp.sum(picked * query_rows.astype(jnp.float32)[:, None, :], axis=-1))
    raw_scores = lax.map(score_device, (cand_dev, query_dev)).reshape(REQS, CANDS)
    scores = raw_scores * score_scale + tower_values[positions]

    def add_grads(device, summed):
        ids = lax.dynamic_index_in_dim(cand_dev, device, 0, False)
        query_rows = lax.dynamic_index_in_dim(query_dev, device, 0, False).astype(jnp.float32)
        cot_rows = lax.dynamic_index_in_dim(cot_dev, device, 0, False).astype(jnp.float32)
        terms = (cot_rows[:, :, None] * query_rows[:, None, :]).reshape(-1, D)
        return summed.at[ids.reshape(-1)].add(terms)
    grad_hidden = lax.fori_loop(0, device_total, add_grads, jnp.zeros((ITEMS, D), jnp.float32)) * score_scale
    grad_preact = pullback(grad_hidden)[0]
    grad_rounded = grad_preact.astype(jnp.bfloat16)
    grad_self = jnp.dot(grad_rounded, self_weight.T, preferred_element_type=jnp.float32)
    back_source = jnp.dot(grad_rounded, neighbor_weight.T, preferred_element_type=jnp.float32).astype(jnp.bfloat16)
    back_grid = back_source.reshape(N_ROW, row_blocks, BLK, D)

    def backward_column(col_index):

        def add_row(row_index, summed):
            source = lax.dynamic_index_in_dim(back_grid, row_index, 0, False)
            tile_set = blocks[row_index, col_index].astype(jnp.float32)
            is_live = (slot_index < counts[row_index, col_index]).astype(jnp.float32)
            gathered = source[block_rows[row_index, col_index]].astype(jnp.float32)
            product = jnp.einsum('nij,nid->njd', tile_set, gathered) * is_live[:, None, None]
            return summed + round_part(jax.ops.segment_sum(product, block_cols[row_index, col_index], col_blocks))
        return lax.fori_loop(0, N_ROW, add_row, jnp.zeros((col_blocks, BLK, D), jnp.float32))
    back_sum = lax.map(backward_column, jnp.arange(N_COL)).reshape(N_COL, N_ROW, ITEMS_DEV, D)
    back_sum = back_sum.transpose(1, 0, 2, 3).reshape(ITEMS, D)
    return (hidden, scores, grad_self + back_sum)
```

```python
import functools

import jax
import jax.numpy as jnp
from jax import lax
from jax.experimental import pallas as pl
from jax.experimental.pallas import tpu as pltpu
from jax.sharding import PartitionSpec as P

norm_eps = 1e-05
f32 = jnp.float32
bf16 = jnp.bfloat16
VMEM_LIMIT = 56 * 1024 * 1024


def dot(a, b, dims=((1,), (0,))):
    return lax.dot_general(a, b, (dims, ((), ())), preferred_element_type=f32)


def block_kernel(
    transpose, chunk, unroll, targets, sources, count, tiles, source, out, total
):
    step = pl.program_id(0)
    target_blocks = out.shape[0]

    @pl.when(step == 0)
    def _():
        total[...] = jnp.zeros_like(total)

    live = jnp.clip(count[0] - step * chunk, 0, chunk)

    def group(index, carry):
        for lane in range(unroll):
            slot = index * unroll + lane
            place = step * chunk + slot
            target = jnp.where(slot < live, targets[place], target_blocks)
            dims = ((0,), (0,)) if transpose else ((1,), (0,))
            total[target] += dot(tiles[slot], source[sources[place]], dims)
        return carry

    lax.fori_loop(0, (live + unroll - 1) // unroll, group, 0)

    @pl.when(step == pl.num_programs(0) - 1)
    def _():
        out[...] = total[0:target_blocks].astype(out.dtype)


def block_products(tiles, targets, sources, count, source, target_blocks, transpose):
    slots, block, _ = tiles.shape
    width = source.shape[-1]
    chunk = min(32, slots)
    shaped = source.reshape(-1, block, width)
    return pl.pallas_call(
        functools.partial(block_kernel, transpose, chunk, 4),
        grid_spec=pltpu.PrefetchScalarGridSpec(
            num_scalar_prefetch=3,
            grid=(slots // chunk,),
            in_specs=[
                pl.BlockSpec((chunk, block, block), lambda i, *_: (i, 0, 0)),
                pl.BlockSpec(shaped.shape, lambda i, *_: (0, 0, 0)),
            ],
            out_specs=pl.BlockSpec((target_blocks, block, width), lambda i, *_: (0, 0, 0)),
            scratch_shapes=[pltpu.VMEM((target_blocks + 1, block, width), f32)],
        ),
        out_shape=jax.ShapeDtypeStruct((target_blocks, block, width), bf16),
        compiler_params=pltpu.CompilerParams(vmem_limit_bytes=VMEM_LIMIT),
        name="block_products",
    )(targets, sources, count, tiles, shaped).reshape(target_blocks * block, width)


def weights_of(ids, cot, weights):
    rows = min(128, weights.shape[0])
    queries = weights.shape[1]

    def part(index, carry):
        start = index * rows
        numbers = lax.broadcasted_iota(jnp.int32, (rows, queries), 0) + start
        acc = jnp.zeros((rows, queries), f32)
        for k in range(ids.shape[0]):
            acc += jnp.where(numbers == ids[k : k + 1, :], cot[k : k + 1, :], 0.0)
        weights[pl.ds(pl.multiple_of(start, rows), rows), :] = acc
        return carry

    lax.fori_loop(0, weights.shape[0] // rows, part, 0)


def picked_scores(ids, table, picks, raw):
    rows = min(128, table.shape[0])
    queries = table.shape[1]
    picks[...] = jnp.zeros_like(picks)

    def part(index, carry):
        start = index * rows
        numbers = lax.broadcasted_iota(jnp.int32, (rows, queries), 0) + start
        values = table[pl.ds(pl.multiple_of(start, rows), rows), :]
        for k in range(ids.shape[0]):
            hit = jnp.where(numbers == ids[k : k + 1, :], values, 0.0)
            picks[k] += jnp.sum(hit.reshape(rows // 8, 8, queries), axis=0)
        return carry

    lax.fori_loop(0, table.shape[0] // rows, part, 0)
    raw[...] = jnp.sum(picks[...], axis=1)


def node_math(items, aggregate, w_self, w_neighbor, bias, gain, weights, queries):
    width = items.shape[1]
    preact = dot(items, w_self) + dot(aggregate.astype(bf16), w_neighbor) + bias
    gate = 1.0 / (1.0 + jnp.exp(-preact))
    active = preact * gate
    scale = lax.rsqrt(jnp.mean(active * active, axis=-1, keepdims=True) + norm_eps)
    hidden = (gain * active * scale).astype(bf16)
    high = weights.astype(bf16)
    low = (weights - high.astype(f32)).astype(bf16)
    grad_hidden = (dot(high, queries) + dot(low, queries)) * (width ** -0.5)
    scaled = gain * grad_hidden
    along = jnp.sum(scaled * active, axis=-1, keepdims=True) * (1.0 / width)
    grad_active = scale * scaled - active * (scale * scale * scale * along)
    grad_preact = grad_active * (gate * (1.0 + preact * (1.0 - gate)))
    return hidden, grad_preact.astype(bf16)


def node_kernel(
    items, aggregate, w_self, w_neighbor, bias, gain, queries, ids, cot,
    hidden, grad_self, back_source, raw, weights, table, picks,
):
    weights_of(ids, cot, weights)
    new, grad = node_math(
        items[...], aggregate[...], w_self[...], w_neighbor[...], bias[...], gain[...],
        weights[...], queries[...],
    )
    hidden[...] = new
    last = ((1,), (1,))
    back_source[...] = dot(grad, w_neighbor[...], last).astype(bf16)
    grad_self[...] = dot(grad, w_self[...], last)
    table[...] = dot(new, queries[...], last)
    picked_scores(ids, table, picks, raw)


def node_step(items, aggregate, w_self, w_neighbor, bias, gain, queries, ids, cot):
    rows, width = items.shape
    requests = queries.shape[0]
    cands = ids.shape[0]
    return pl.pallas_call(
        node_kernel,
        out_shape=(
            jax.ShapeDtypeStruct((rows, width), bf16),
            jax.ShapeDtypeStruct((rows, width), f32),
            jax.ShapeDtypeStruct((rows, width), bf16),
            jax.ShapeDtypeStruct((cands, requests), f32),
        ),
        scratch_shapes=[
            pltpu.VMEM((rows, requests), f32),
            pltpu.VMEM((rows, requests), f32),
            pltpu.VMEM((cands, 8, requests), f32),
        ],
        compiler_params=pltpu.CompilerParams(vmem_limit_bytes=VMEM_LIMIT),
        name="node_step",
    )(items, aggregate, w_self, w_neighbor, bias[None], gain[None], queries, ids, cot)


def body(
    item_features,
    self_weight,
    neighbor_weight,
    layer_bias,
    norm_gain,
    blocks,
    block_rows,
    block_cols,
    counts,
    queries,
    candidates,
    positions,
    position_table,
    tower_weight,
    score_cotangent,
):
    rows_dev, width = item_features.shape
    tiles = blocks[0, 0]
    block = tiles.shape[1]
    cands = candidates.shape[1]
    col_count = lax.axis_size("col")
    row_count = lax.axis_size("row")
    column_items = lax.all_gather(item_features, "row", axis=0, tiled=True)
    packed = jnp.concatenate(
        [queries.astype(f32), candidates.astype(f32), score_cotangent.astype(f32)], axis=1
    )
    packed = lax.all_gather(packed, "row", axis=0, tiled=True)
    all_queries = packed[:, :width].astype(bf16)
    all_ids = packed[:, width : width + cands].astype(jnp.int32).T
    all_cot = packed[:, width + cands :].T
    my_piece = lax.axis_index("row") * col_count + lax.axis_index("col")
    local_ids = jnp.where(all_ids // rows_dev == my_piece, all_ids % rows_dev, -1)

    parts = block_products(
        tiles, block_rows[0, 0], block_cols[0, 0], counts[0],
        column_items, col_count * rows_dev // block, False,
    )
    aggregate = lax.psum_scatter(parts, "col", scatter_dimension=0, tiled=True)
    hidden, grad_self, back_source, raw = node_step(
        item_features, aggregate, self_weight, neighbor_weight, layer_bias, norm_gain,
        all_queries, local_ids, all_cot,
    )
    range_source = lax.all_gather(back_source, "col", axis=0, tiled=True)
    back_parts = block_products(
        tiles, block_cols[0, 0], block_rows[0, 0], counts[0],
        range_source, row_count * rows_dev // block, True,
    )
    raw_scores = lax.psum_scatter(raw.T, "row", scatter_dimension=0, tiled=True)
    tower_values = jnp.sum(jax.nn.relu(position_table) * tower_weight, axis=-1)
    position_hits = positions[..., None] == jnp.arange(tower_values.shape[0])
    scores = raw_scores * width ** (-0.5) + jnp.sum(
        jnp.where(position_hits, tower_values, 0.0), axis=-1
    )
    back_sum = lax.psum_scatter(back_parts, "row", scatter_dimension=0, tiled=True)
    return (hidden, scores, grad_self + back_sum.astype(f32))


def solution(mesh):
    in_specs = (
        P(("row", "col"), None),
        P(),
        P(),
        P(),
        P(),
        P("row", "col", None, None, None),
        P("row", "col", None),
        P("row", "col", None),
        P("row", "col"),
        P(("row", "col"), None),
        P(("row", "col"), None),
        P(("row", "col"), None),
        P(),
        P(),
        P(("row", "col"), None),
    )
    out_specs = (P(("row", "col"), None), P(("row", "col"), None), P(("row", "col"), None))
    return jax.shard_map(body, mesh=mesh, in_specs=in_specs, out_specs=out_specs, check_vma=False)
```

```python
import functools

import jax
import jax.numpy as jnp
from jax import lax
from jax.experimental import pallas as pl
from jax.experimental.pallas import tpu as pltpu
from jax.sharding import PartitionSpec as P

norm_eps = 1e-05
f32 = jnp.float32
bf16 = jnp.bfloat16
VMEM_LIMIT = 56 * 1024 * 1024


def dot(a, b, dims=((1,), (0,))):
    return lax.dot_general(a, b, (dims, ((), ())), preferred_element_type=f32)


def block_kernel(
    transpose, chunk, unroll, targets, sources, count, tiles, source, out, total
):
    step = pl.program_id(0)
    target_blocks = out.shape[0]

    @pl.when(step == 0)
    def _():
        total[...] = jnp.zeros_like(total)

    live = jnp.clip(count[0] - step * chunk, 0, chunk)

    def group(index, carry):
        for lane in range(unroll):
            slot = index * unroll + lane
            place = step * chunk + slot
            target = jnp.where(slot < live, targets[place], target_blocks)
            dims = ((0,), (0,)) if transpose else ((1,), (0,))
            total[target] += dot(tiles[slot], source[sources[place]], dims)
        return carry

    lax.fori_loop(0, (live + unroll - 1) // unroll, group, 0)

    @pl.when(step == pl.num_programs(0) - 1)
    def _():
        out[...] = total[0:target_blocks].astype(out.dtype)


def block_products(tiles, targets, sources, count, source, target_blocks, transpose):
    slots, block, _ = tiles.shape
    width = source.shape[-1]
    chunk = min(32, slots)
    shaped = source.reshape(-1, block, width)
    return pl.pallas_call(
        functools.partial(block_kernel, transpose, chunk, 4),
        grid_spec=pltpu.PrefetchScalarGridSpec(
            num_scalar_prefetch=3,
            grid=(slots // chunk,),
            in_specs=[
                pl.BlockSpec((chunk, block, block), lambda i, *_: (i, 0, 0)),
                pl.BlockSpec(shaped.shape, lambda i, *_: (0, 0, 0)),
            ],
            out_specs=pl.BlockSpec((target_blocks, block, width), lambda i, *_: (0, 0, 0)),
            scratch_shapes=[pltpu.VMEM((target_blocks + 1, block, width), f32)],
        ),
        out_shape=jax.ShapeDtypeStruct((target_blocks, block, width), bf16),
        compiler_params=pltpu.CompilerParams(vmem_limit_bytes=VMEM_LIMIT),
        name="block_products",
    )(targets, sources, count, tiles, shaped).reshape(target_blocks * block, width)


def node_math(items, aggregate, w_self, w_neighbor, bias, gain, weights, queries):
    width = items.shape[1]
    preact = dot(items, w_self) + dot(aggregate.astype(bf16), w_neighbor) + bias
    gate = 1.0 / (1.0 + jnp.exp(-preact))
    active = preact * gate
    scale = lax.rsqrt(jnp.mean(active * active, axis=-1, keepdims=True) + norm_eps)
    hidden = (gain * active * scale).astype(bf16)
    high = weights.astype(bf16)
    low = (weights - high.astype(f32)).astype(bf16)
    grad_hidden = (dot(high, queries) + dot(low, queries)) * (width ** -0.5)
    scaled = gain * grad_hidden
    along = jnp.sum(scaled * active, axis=-1, keepdims=True) * (1.0 / width)
    grad_active = scale * scaled - active * (scale * scale * scale * along)
    grad_preact = grad_active * (gate * (1.0 + preact * (1.0 - gate)))
    return hidden, grad_preact.astype(bf16)


def remote(src, dst, send, recv, place):
    return pltpu.make_async_remote_copy(
        src_ref=src, dst_ref=dst, send_sem=send, recv_sem=recv,
        device_id=place, device_id_type=pl.DeviceIdType.MESH,
    )


def greet(places):
    barrier = pltpu.get_barrier_semaphore()
    for place in places:
        pl.semaphore_signal(
            barrier, inc=1, device_id=place, device_id_type=pl.DeviceIdType.MESH
        )
    pl.semaphore_wait(barrier, len(places))


def row_places(chips):
    me = lax.axis_index("row")
    core = lax.rem(me, 2)
    chip = me // 2
    ahead = [lax.rem(chip + i, chips) for i in range(chips)]
    behind = [lax.rem(chip + chips - i, chips) for i in range(chips)]
    return me, core, ahead, behind


def gather_kernel(chips, *refs):
    arrays = len(refs) // 2 - 1
    inputs, outputs = refs[:arrays], refs[arrays : 2 * arrays]
    send, recv = refs[2 * arrays :]
    me, core, ahead, behind = row_places(chips)
    sibling = {"row": me + 1 - 2 * core}
    peers = [{"row": ahead[i] * 2 + core} for i in range(chips)]
    greet(peers[1:] + [sibling])
    copies = []
    for n in range(arrays):
        for i in range(1, chips):
            copy = remote(
                inputs[n], outputs[n].at[me], send.at[n, i], recv.at[n, i], peers[i]
            )
            copy.start()
            copies.append(copy)
    for n in range(arrays):
        copy = remote(
            inputs[n], outputs[n].at[me], send.at[n, chips], recv.at[n, chips], sibling
        )
        copy.start()
        copies.append(copy)
    own = [
        pltpu.make_async_copy(inputs[n], outputs[n].at[me], send.at[n, 0])
        for n in range(arrays)
    ]
    for copy in own:
        copy.start()
    forwards = []
    for n in reversed(range(arrays)):
        for i in range(1, chips):
            copies[n * (chips - 1) + i - 1].wait_recv()
            piece = outputs[n].at[behind[i] * 2 + core]
            copy = remote(
                piece, piece, send.at[n, chips + i], recv.at[n, chips + i], sibling
            )
            copy.start()
            forwards.append(copy)
    for copy in copies[arrays * (chips - 1) :]:
        copy.wait_recv()
    for copy in forwards:
        copy.wait_recv()
    for copy in copies + forwards:
        copy.wait_send()
    for copy in own:
        copy.wait()


def gather_rows(row_count, *arrays):
    chips = row_count // 2
    return pl.pallas_call(
        functools.partial(gather_kernel, chips),
        out_shape=tuple(
            jax.ShapeDtypeStruct((row_count,) + array.shape, array.dtype) for array in arrays
        ),
        in_specs=[pl.BlockSpec(memory_space=pl.ANY)] * len(arrays),
        out_specs=tuple(pl.BlockSpec(memory_space=pl.ANY) for _ in arrays),
        scratch_shapes=[
            pltpu.SemaphoreType.DMA((len(arrays), 2 * chips)),
            pltpu.SemaphoreType.DMA((len(arrays), 2 * chips)),
        ],
        compiler_params=pltpu.CompilerParams(
            collective_id=0, has_side_effects=True, vmem_limit_bytes=VMEM_LIMIT
        ),
        name="gather_rows",
    )(*arrays)


def scatter_kernel(
    chips, scale, parts, raw, grad_self, position_scores, grads, scores,
    near, sums, far, near_raw, sums_raw, far_raw, send, recv,
):
    me, core, ahead, behind = row_places(chips)
    sibling = {"row": me + 1 - 2 * core}
    peers = [{"row": ahead[i] * 2 + core} for i in range(chips)]
    greet(peers[1:] + [sibling])
    order = list(range(1, chips)) + [0]
    arrays = ((parts, near, sums, far), (raw, near_raw, sums_raw, far_raw))
    first = {}
    for i in order:
        for n, (mine, inbox, _, _) in enumerate(arrays):
            copy = remote(
                mine.at[ahead[i] * 2 + 1 - core], inbox.at[i],
                send.at[n, i], recv.at[n, i], sibling,
            )
            copy.start()
            first[n, i] = copy
    second = []
    for i in order:
        for n, (mine, inbox, summed, outbox) in enumerate(arrays):
            first[n, i].wait_recv()
            value = mine[ahead[i] * 2 + core].astype(f32) + inbox[i].astype(f32)
            if i == 0:
                if n == 0:
                    grads[...] = grad_self[...] + value
                else:
                    scores[...] = value
            else:
                summed[i] = value.astype(summed.dtype)
                copy = remote(
                    summed.at[i], outbox.at[i],
                    send.at[n, chips + i], recv.at[n, chips + i], peers[i],
                )
                copy.start()
                second.append((n, i, copy))
    for n, i, copy in second:
        copy.wait_recv()
        if n == 0:
            grads[...] += far[i].astype(f32)
        else:
            scores[...] += far_raw[i]
    scores[...] = scores[...] * scale + position_scores[...]
    for copy in first.values():
        copy.wait_send()
    for _, _, copy in second:
        copy.wait_send()


def scatter_rows(row_count, parts, raw, grad_self, position_scores, scale):
    chips = row_count // 2
    part = parts.shape[1:]
    part_raw = raw.shape[1:]
    return pl.pallas_call(
        functools.partial(scatter_kernel, chips, scale),
        out_shape=(
            jax.ShapeDtypeStruct(grad_self.shape, f32),
            jax.ShapeDtypeStruct(position_scores.shape, f32),
        ),
        in_specs=[pl.BlockSpec(memory_space=pltpu.VMEM)] * 4,
        out_specs=(pl.BlockSpec(memory_space=pltpu.VMEM),) * 2,
        scratch_shapes=[pltpu.VMEM((chips,) + part, bf16)] * 3
        + [pltpu.VMEM((chips,) + part_raw, f32)] * 3
        + [
            pltpu.SemaphoreType.DMA((2, 2 * chips)),
            pltpu.SemaphoreType.DMA((2, 2 * chips)),
        ],
        compiler_params=pltpu.CompilerParams(
            collective_id=1, has_side_effects=True, vmem_limit_bytes=VMEM_LIMIT
        ),
        name="scatter_rows",
    )(parts, raw, grad_self, position_scores)


def node_kernel(
    cols, steps, items, aggregate, w_self, w_neighbor, bias, gain, queries, ids, cot,
    hidden, grad_self, source, raw,
    grads, table, picks, send, recv,
):
    me = lax.axis_index("col")
    rows = items.shape[0] // steps
    width = items.shape[1]
    ways = (1, -1)
    is_inner = (me < cols - 1, me > 0)
    barrier = pltpu.get_barrier_semaphore()
    for way in range(2):

        @pl.when(is_inner[way])
        def _():
            pl.semaphore_signal(
                barrier, inc=1, device_id={"col": me + ways[way]},
                device_id_type=pl.DeviceIdType.MESH,
            )

    pl.semaphore_wait(
        barrier, is_inner[0].astype(jnp.int32) + is_inner[1].astype(jnp.int32)
    )

    def hop(way, far, j, piece):
        ref = source.at[piece, pl.ds(j * rows, rows)]
        return remote(
            ref, ref, send.at[way, far, j], recv.at[way, far, j], {"col": me + ways[way]}
        )

    def outgoing(way, far, j):
        return hop(way, far, j, me - ways[way] * far)

    def incoming(way, far, j):
        return hop(way, far, j, me - ways[way] * (far + 1))

    def has(way, far):
        return me >= far if way == 0 else me + far < cols

    def node_part(j):
        span = pl.ds(j * rows, rows)
        weights = part_weights(ids, cot, j * rows, rows)
        new, grad = node_math(
            items[span, :], aggregate[span, :], w_self[...], w_neighbor[...], bias[...],
            gain[...], weights, queries[...],
        )
        hidden[span, :] = new
        grads[span, :] = grad
        source[me, span, :] = dot(grad, w_neighbor[...], ((1,), (1,))).astype(bf16)
        for way in range(2):

            @pl.when(is_inner[way])
            def _():
                outgoing(way, 0, j).start()

    def late_part(j):
        span = pl.ds(j * rows, rows)
        last = ((1,), (1,))
        grad_self[span, :] = dot(grads[span, :], w_self[...], last)
        table[...] = dot(hidden[span, :], queries[...], last)
        part_scores(ids, table, j * rows, rows, picks)

    picks[...] = jnp.zeros_like(picks)
    for j in range(steps):
        node_part(j)
    for far in range(cols - 1):
        for j in range(steps):
            if far == 0:
                late_part(j)
            for way in range(2):

                @pl.when(has(way, far + 1))
                def _():
                    incoming(way, far, j).wait_recv()

                if far + 1 < cols - 1:

                    @pl.when(has(way, far + 1) & is_inner[way])
                    def _():
                        outgoing(way, far + 1, j).start()

    raw[...] = jnp.sum(picks[...], axis=1).T
    for far in range(cols - 1):
        for j in range(steps):
            for way in range(2):

                @pl.when(has(way, far) & is_inner[way])
                def _():
                    outgoing(way, far, j).wait_send()


def part_weights(ids, cot, start, rows):
    queries = ids.shape[1]
    numbers = lax.broadcasted_iota(jnp.int32, (rows, queries), 0) + start
    acc = jnp.zeros((rows, queries), f32)
    for k in range(ids.shape[0]):
        acc += jnp.where(numbers == ids[k : k + 1, :], cot[k : k + 1, :], 0.0)
    return acc


def part_scores(ids, table, start, rows, picks):
    queries = ids.shape[1]
    numbers = lax.broadcasted_iota(jnp.int32, (rows, queries), 0) + start
    values = table[...]
    for k in range(ids.shape[0]):
        hit = jnp.where(numbers == ids[k : k + 1, :], values, 0.0)
        picks[k] += jnp.sum(hit.reshape(rows // 8, 8, queries), axis=0)


def node_step(cols, items, aggregate, w_self, w_neighbor, bias, gain, queries, ids, cot):
    rows, width = items.shape
    requests = queries.shape[0]
    cands = ids.shape[0]
    steps = max(rows // 128, 1)
    return pl.pallas_call(
        functools.partial(node_kernel, cols, steps),
        out_shape=(
            jax.ShapeDtypeStruct((rows, width), bf16),
            jax.ShapeDtypeStruct((rows, width), f32),
            jax.ShapeDtypeStruct((cols, rows, width), bf16),
            jax.ShapeDtypeStruct((requests, cands), f32),
        ),
        in_specs=[pl.BlockSpec(memory_space=pltpu.VMEM)] * 9,
        out_specs=(pl.BlockSpec(memory_space=pltpu.VMEM),) * 4,
        scratch_shapes=[
            pltpu.VMEM((rows, width), bf16),
            pltpu.VMEM((rows // steps, requests), f32),
            pltpu.VMEM((cands, 8, requests), f32),
            pltpu.SemaphoreType.DMA((2, cols, steps)),
            pltpu.SemaphoreType.DMA((2, cols, steps)),
        ],
        compiler_params=pltpu.CompilerParams(
            collective_id=2, has_side_effects=True, vmem_limit_bytes=VMEM_LIMIT
        ),
        name="node_step",
    )(items, aggregate, w_self, w_neighbor, bias[None], gain[None], queries, ids, cot)


def body(
    item_features,
    self_weight,
    neighbor_weight,
    layer_bias,
    norm_gain,
    blocks,
    block_rows,
    block_cols,
    counts,
    queries,
    candidates,
    positions,
    position_table,
    tower_weight,
    score_cotangent,
):
    rows_dev, width = item_features.shape
    tiles = blocks[0, 0]
    block = tiles.shape[1]
    cands = candidates.shape[1]
    col_count = lax.axis_size("col")
    row_count = lax.axis_size("row")
    packed = jnp.concatenate(
        [queries.astype(f32), candidates.astype(f32), score_cotangent.astype(f32)], axis=1
    )
    column_items, packed = gather_rows(row_count, item_features, packed)
    packed = packed.reshape(-1, width + 2 * cands)
    all_queries = packed[:, :width].astype(bf16)
    all_ids = packed[:, width : width + cands].astype(jnp.int32).T
    all_cot = packed[:, width + cands :].T
    my_piece = lax.axis_index("row") * col_count + lax.axis_index("col")
    local_ids = jnp.where(all_ids // rows_dev == my_piece, all_ids % rows_dev, -1)
    tower_values = jnp.sum(jax.nn.relu(position_table) * tower_weight, axis=-1)
    position_hits = positions[..., None] == jnp.arange(tower_values.shape[0])
    position_scores = jnp.sum(jnp.where(position_hits, tower_values, 0.0), axis=-1)

    parts = block_products(
        tiles, block_rows[0, 0], block_cols[0, 0], counts[0],
        column_items, col_count * rows_dev // block, False,
    )
    aggregate = lax.psum_scatter(parts, "col", scatter_dimension=0, tiled=True)
    hidden, grad_self, range_source, raw = node_step(
        col_count, item_features, aggregate, self_weight, neighbor_weight, layer_bias,
        norm_gain, all_queries, local_ids, all_cot,
    )
    back_parts = block_products(
        tiles, block_cols[0, 0], block_rows[0, 0], counts[0],
        range_source, row_count * rows_dev // block, True,
    )
    item_grads, scores = scatter_rows(
        row_count,
        back_parts.reshape(row_count, rows_dev, width),
        raw.reshape(row_count, -1, cands),
        grad_self,
        position_scores,
        width ** (-0.5),
    )
    return (hidden, scores, item_grads)


def solution(mesh):
    in_specs = (
        P(("row", "col"), None),
        P(),
        P(),
        P(),
        P(),
        P("row", "col", None, None, None),
        P("row", "col", None),
        P("row", "col", None),
        P("row", "col"),
        P(("row", "col"), None),
        P(("row", "col"), None),
        P(("row", "col"), None),
        P(),
        P(),
        P(("row", "col"), None),
    )
    out_specs = (P(("row", "col"), None), P(("row", "col"), None), P(("row", "col"), None))
    return jax.shard_map(body, mesh=mesh, in_specs=in_specs, out_specs=out_specs, check_vma=False)
```

```python
import functools

import jax
import jax.numpy as jnp
from jax import lax
from jax.experimental import pallas as pl
from jax.experimental.pallas import tpu as pltpu
from jax.sharding import PartitionSpec as P

norm_eps = 1e-05
f32 = jnp.float32
bf16 = jnp.bfloat16
VMEM_LIMIT = 56 * 1024 * 1024


def dot(a, b, dims=((1,), (0,))):
    return lax.dot_general(a, b, (dims, ((), ())), preferred_element_type=f32)


def block_kernel(
    transpose, chunk, unroll, targets, sources, count, tiles, source, *refs
):
    kept = (len(refs) - 5) // 2
    out = refs[kept]
    total, held, held_source, arrived, source_arrived = refs[2 * kept + 1 :]
    target_blocks = out.shape[0]
    chunks = tiles.shape[0] // chunk
    live = count[0]

    def fetch(index):
        span = pl.ds(index * chunk, chunk)
        return pltpu.make_async_copy(tiles.at[span], held.at[span], arrived.at[index])

    fetch_source = pltpu.make_async_copy(source, held_source, source_arrived)
    fetch_source.start()
    for index in range(chunks):

        @pl.when(index * chunk < live)
        def _():
            fetch(index).start()

    total[...] = jnp.zeros_like(total)
    for n in range(kept):
        refs[kept + 1 + n][...] = refs[n][...]
    fetch_source.wait()

    def group(index, carry):
        for lane in range(unroll):
            place = index * unroll + lane
            target = jnp.where(place < live, targets[place], target_blocks)
            dims = ((0,), (0,)) if transpose else ((1,), (0,))
            total[target] += dot(held[place], held_source[sources[place]], dims)
        return carry

    def part(index, carry):
        fetch(index).wait()
        start = index * (chunk // unroll)
        stop = jnp.minimum(start + chunk // unroll, (live + unroll - 1) // unroll)
        return lax.fori_loop(start, stop, group, carry)

    lax.fori_loop(0, (live + chunk - 1) // chunk, part, 0)
    out[...] = total[0:target_blocks].astype(out.dtype)


def block_products(tiles, targets, sources, count, source, target_blocks, transpose, kept=()):
    slots, block, _ = tiles.shape
    width = source.shape[-1]
    chunk = min(16, slots)
    shaped = source.reshape(-1, block, width)
    whole = pl.BlockSpec(memory_space=pltpu.VMEM)
    scalars = pl.BlockSpec(memory_space=pltpu.SMEM)
    stays = pl.BlockSpec(memory_space=pl.ANY)
    out, *rest = pl.pallas_call(
        functools.partial(block_kernel, transpose, chunk, min(8, chunk)),
        in_specs=[scalars] * 3 + [stays] * 2 + [whole] * len(kept),
        out_specs=(whole,) * (1 + len(kept)),
        scratch_shapes=[
            pltpu.VMEM((target_blocks + 1, block, width), f32),
            pltpu.VMEM(tiles.shape, bf16),
            pltpu.VMEM(shaped.shape, bf16),
            pltpu.SemaphoreType.DMA((slots // chunk,)),
            pltpu.SemaphoreType.DMA,
        ],
        out_shape=(jax.ShapeDtypeStruct((target_blocks, block, width), bf16),)
        + tuple(jax.ShapeDtypeStruct(array.shape, array.dtype) for array in kept),
        compiler_params=pltpu.CompilerParams(vmem_limit_bytes=VMEM_LIMIT),
        name="block_products",
    )(targets, sources, count, tiles, shaped, *kept)
    return (out.reshape(target_blocks * block, width), *rest)


def node_math(base, aggregate, w_neighbor, gain, weights, queries):
    width = base.shape[1]
    preact = base + dot(aggregate.astype(bf16), w_neighbor)
    gate = 1.0 / (1.0 + jnp.exp(-preact))
    active = preact * gate
    scale = lax.rsqrt(jnp.mean(active * active, axis=-1, keepdims=True) + norm_eps)
    hidden = (gain * active * scale).astype(bf16)
    high = weights.astype(bf16)
    low = (weights - high.astype(f32)).astype(bf16)
    grad_hidden = (dot(high, queries) + dot(low, queries)) * (width ** -0.5)
    scaled = gain * grad_hidden
    along = jnp.sum(scaled * active, axis=-1, keepdims=True) * (1.0 / width)
    grad_active = scale * scaled - active * (scale * scale * scale * along)
    grad_preact = grad_active * (gate * (1.0 + preact * (1.0 - gate)))
    return hidden, grad_preact.astype(bf16)


def remote(src, dst, send, recv, place):
    return pltpu.make_async_remote_copy(
        src_ref=src, dst_ref=dst, send_sem=send, recv_sem=recv,
        device_id=place, device_id_type=pl.DeviceIdType.MESH,
    )


def greet(places):
    barrier = pltpu.get_barrier_semaphore()
    for place in places:
        pl.semaphore_signal(
            barrier, inc=1, device_id=place, device_id_type=pl.DeviceIdType.MESH
        )
    pl.semaphore_wait(barrier, len(places))


def row_places(chips):
    me = lax.axis_index("row")
    core = lax.rem(me, 2)
    chip = me // 2
    ahead = [lax.rem(chip + i, chips) for i in range(chips)]
    behind = [lax.rem(chip + chips - i, chips) for i in range(chips)]
    return me, core, ahead, behind


def gather_kernel(
    chips, items, queries, candidates, cotangent, all_items, all_packed, packed, send, recv
):
    arrays = 2
    inputs, outputs = (items, packed), (all_items, all_packed)
    me, core, ahead, behind = row_places(chips)
    sibling = {"row": me + 1 - 2 * core}
    peers = [{"row": ahead[i] * 2 + core} for i in range(chips)]
    packed[...] = jnp.concatenate(
        [ref[...].astype(f32) for ref in (queries, candidates, cotangent)], axis=1
    )
    greet(peers[1:] + [sibling])
    copies = []
    for n in range(arrays):
        for i in range(1, chips):
            copy = remote(
                inputs[n], outputs[n].at[me], send.at[n, i], recv.at[n, i], peers[i]
            )
            copy.start()
            copies.append(copy)
    for n in range(arrays):
        copy = remote(
            inputs[n], outputs[n].at[me], send.at[n, chips], recv.at[n, chips], sibling
        )
        copy.start()
        copies.append(copy)
    own = [
        pltpu.make_async_copy(inputs[n], outputs[n].at[me], send.at[n, 0])
        for n in range(arrays)
    ]
    for copy in own:
        copy.start()
    forwards = []
    for n in reversed(range(arrays)):
        for i in range(1, chips):
            copies[n * (chips - 1) + i - 1].wait_recv()
            piece = outputs[n].at[behind[i] * 2 + core]
            copy = remote(
                piece, piece, send.at[n, chips + i], recv.at[n, chips + i], sibling
            )
            copy.start()
            forwards.append(copy)
    for copy in copies[arrays * (chips - 1) :]:
        copy.wait_recv()
    for copy in forwards:
        copy.wait_recv()
    for copy in copies + forwards:
        copy.wait_send()
    for copy in own:
        copy.wait()


def gather_rows(row_count, items, queries, candidates, cotangent):
    chips = row_count // 2
    small = (queries, candidates, cotangent)
    packed = (queries.shape[0], sum(array.shape[1] for array in small))
    return pl.pallas_call(
        functools.partial(gather_kernel, chips),
        out_shape=(
            jax.ShapeDtypeStruct((row_count,) + items.shape, items.dtype),
            jax.ShapeDtypeStruct((row_count,) + packed, f32),
        ),
        in_specs=[pl.BlockSpec(memory_space=pl.ANY)]
        + [pl.BlockSpec(memory_space=pltpu.VMEM)] * 3,
        out_specs=(pl.BlockSpec(memory_space=pl.ANY),) * 2,
        scratch_shapes=[
            pltpu.VMEM(packed, f32),
            pltpu.SemaphoreType.DMA((2, 2 * chips)),
            pltpu.SemaphoreType.DMA((2, 2 * chips)),
        ],
        compiler_params=pltpu.CompilerParams(
            collective_id=0, has_side_effects=True, vmem_limit_bytes=VMEM_LIMIT
        ),
        name="gather_rows",
    )(items, *small)


def scatter_kernel(
    chips, scale, parts, raw, grad_self, position_scores, grads, scores,
    near, sums, far, near_raw, sums_raw, far_raw, send, recv,
):
    me, core, ahead, behind = row_places(chips)
    sibling = {"row": me + 1 - 2 * core}
    peers = [{"row": ahead[i] * 2 + core} for i in range(chips)]
    greet(peers[1:] + [sibling])
    order = list(range(1, chips)) + [0]
    arrays = ((parts, near, sums, far), (raw, near_raw, sums_raw, far_raw))
    first = {}
    for i in order:
        for n, (mine, inbox, _, _) in enumerate(arrays):
            copy = remote(
                mine.at[ahead[i] * 2 + 1 - core], inbox.at[i],
                send.at[n, i], recv.at[n, i], sibling,
            )
            copy.start()
            first[n, i] = copy
    second = []
    for i in order:
        for n, (mine, inbox, summed, outbox) in enumerate(arrays):
            first[n, i].wait_recv()
            value = mine[ahead[i] * 2 + core].astype(f32) + inbox[i].astype(f32)
            if i == 0:
                if n == 0:
                    grads[...] = grad_self[...] + value
                else:
                    scores[...] = value
            else:
                summed[i] = value.astype(summed.dtype)
                copy = remote(
                    summed.at[i], outbox.at[i],
                    send.at[n, chips + i], recv.at[n, chips + i], peers[i],
                )
                copy.start()
                second.append((n, i, copy))
    for n, i, copy in second:
        copy.wait_recv()
        if n == 0:
            grads[...] += far[i].astype(f32)
        else:
            scores[...] += far_raw[i]
    scores[...] = scores[...] * scale + position_scores[...]
    for copy in first.values():
        copy.wait_send()
    for _, _, copy in second:
        copy.wait_send()


def scatter_rows(row_count, parts, raw, grad_self, position_scores, scale):
    chips = row_count // 2
    part = parts.shape[1:]
    part_raw = raw.shape[1:]
    return pl.pallas_call(
        functools.partial(scatter_kernel, chips, scale),
        out_shape=(
            jax.ShapeDtypeStruct(grad_self.shape, f32),
            jax.ShapeDtypeStruct(position_scores.shape, f32),
        ),
        in_specs=[pl.BlockSpec(memory_space=pltpu.VMEM)] * 4,
        out_specs=(pl.BlockSpec(memory_space=pltpu.VMEM),) * 2,
        scratch_shapes=[pltpu.VMEM((chips,) + part, bf16)] * 3
        + [pltpu.VMEM((chips,) + part_raw, f32)] * 3
        + [
            pltpu.SemaphoreType.DMA((2, 2 * chips)),
            pltpu.SemaphoreType.DMA((2, 2 * chips)),
        ],
        compiler_params=pltpu.CompilerParams(
            collective_id=1, has_side_effects=True, vmem_limit_bytes=VMEM_LIMIT
        ),
        name="scatter_rows",
    )(parts, raw, grad_self, position_scores)


def node_kernel(
    cols, steps, items, parts, w_self, w_neighbor, bias, gain, packed,
    hidden, grad_self, source, raw,
    grads, table, picks, queries, ids, cot, weights, base, aggregate, inbox, outbox,
    send, recv, sum_send, sum_recv,
):
    me = lax.axis_index("col")
    piece = lax.axis_index("row") * cols + me
    first_item = piece * items.shape[0]
    cands = ids.shape[0]
    rows = items.shape[0] // steps
    width = items.shape[1]
    ways = (1, -1)
    is_inner = (me < cols - 1, me > 0)
    barrier = pltpu.get_barrier_semaphore()
    for way in range(2):

        @pl.when(is_inner[way])
        def _():
            pl.semaphore_signal(
                barrier, inc=1, device_id={"col": me + ways[way]},
                device_id_type=pl.DeviceIdType.MESH,
            )

    pl.semaphore_wait(
        barrier, is_inner[0].astype(jnp.int32) + is_inner[1].astype(jnp.int32)
    )

    def hop(way, far, j, piece):
        ref = source.at[piece, pl.ds(j * rows, rows)]
        return remote(
            ref, ref, send.at[way, far, j], recv.at[way, far, j], {"col": me + ways[way]}
        )

    def outgoing(way, far, j):
        return hop(way, far, j, me - ways[way] * far)

    def incoming(way, far, j):
        return hop(way, far, j, me - ways[way] * (far + 1))

    def has(way, far):
        return me >= far if way == 0 else me + far < cols

    def sum_hop(way, dest, j, ref):
        return remote(
            ref.at[pl.ds(j * rows, rows)], inbox.at[way, dest, pl.ds(j * rows, rows)],
            sum_send.at[way, dest, j], sum_recv.at[way, dest, j], {"col": me + ways[way]},
        )

    def is_before(way, dest):
        return me < dest if way == 0 else me > dest

    def sum_part(way, dest, j):
        span = pl.ds(j * rows, rows)
        is_end = me == (0 if way == 0 else cols - 1)

        @pl.when(is_end)
        def _():
            sum_hop(way, dest, j, parts.at[dest]).start()

        @pl.when(is_before(way, dest) & jnp.logical_not(is_end))
        def _():
            sum_hop(way, dest, j, parts.at[dest]).wait_recv()
            outbox[way, dest, span, :] = (
                parts[dest, span, :].astype(f32) + inbox[way, dest, span, :].astype(f32)
            ).astype(bf16)
            sum_hop(way, dest, j, outbox.at[way, dest]).start()

    for t in range(cols - 1):
        for j in range(steps):
            sum_part(0, cols - 1 - t, j)
            sum_part(1, t, j)

    queries[...] = packed[:, :width].astype(bf16)
    tail = packed[:, width:].T
    ids[...] = tail[:cands]
    cot[...] = tail[cands:]
    for j in range(steps):
        span = pl.ds(j * rows, rows)
        weights[span, :] = part_weights(ids, cot, first_item + j * rows, rows)
        base[span, :] = dot(items[span, :], w_self[...]) + bias[...]

    def node_part(j):
        span = pl.ds(j * rows, rows)
        aggregate[...] = parts[me, span, :].astype(f32)
        for way in range(2):

            @pl.when(is_inner[1 - way])
            def _():
                sum_hop(way, me, j, parts.at[me]).wait_recv()
                aggregate[...] += inbox[way, me, span, :].astype(f32)

        new, grad = node_math(
            base[span, :], aggregate[...], w_neighbor[...], gain[...], weights[span, :],
            queries[...],
        )
        hidden[span, :] = new
        grads[span, :] = grad
        source[me, span, :] = dot(grad, w_neighbor[...], ((1,), (1,))).astype(bf16)
        for way in range(2):

            @pl.when(is_inner[way])
            def _():
                outgoing(way, 0, j).start()

    def late_part(j):
        span = pl.ds(j * rows, rows)
        last = ((1,), (1,))
        grad_self[span, :] = dot(grads[span, :], w_self[...], last)
        table[...] = dot(hidden[span, :], queries[...], last)
        part_scores(ids, table, first_item + j * rows, rows, picks)

    picks[...] = jnp.zeros_like(picks)
    for j in range(steps):
        node_part(j)
    for far in range(cols - 1):
        for j in range(steps):
            if far == 0:
                late_part(j)
            for way in range(2):

                @pl.when(has(way, far + 1))
                def _():
                    incoming(way, far, j).wait_recv()

                if far + 1 < cols - 1:

                    @pl.when(has(way, far + 1) & is_inner[way])
                    def _():
                        outgoing(way, far + 1, j).start()

    raw[...] = jnp.sum(picks[...], axis=1).T
    for far in range(cols - 1):
        for j in range(steps):
            for way in range(2):

                @pl.when(has(way, far) & is_inner[way])
                def _():
                    outgoing(way, far, j).wait_send()

    for dest in range(cols):
        for j in range(steps):
            for way in range(2):

                @pl.when(is_before(way, dest))
                def _():
                    sum_hop(way, dest, j, parts.at[dest]).wait_send()


def part_weights(ids, cot, start, rows):
    queries = ids.shape[1]
    numbers = (lax.broadcasted_iota(jnp.int32, (rows, queries), 0) + start).astype(f32)
    acc = jnp.zeros((rows, queries), f32)
    for k in range(ids.shape[0]):
        acc += jnp.where(numbers == ids[k : k + 1, :], cot[k : k + 1, :], 0.0)
    return acc


def part_scores(ids, table, start, rows, picks):
    queries = ids.shape[1]
    numbers = (lax.broadcasted_iota(jnp.int32, (rows, queries), 0) + start).astype(f32)
    values = table[...]
    for k in range(ids.shape[0]):
        hit = jnp.where(numbers == ids[k : k + 1, :], values, 0.0)
        picks[k] += jnp.sum(hit.reshape(rows // 8, 8, queries), axis=0)


def node_step(cols, items, parts, w_self, w_neighbor, bias, gain, packed, cands):
    rows, width = items.shape
    requests = packed.shape[0]
    steps = max(rows // 128, 1)
    moves = pltpu.SemaphoreType.DMA((2, cols, steps))
    return pl.pallas_call(
        functools.partial(node_kernel, cols, steps),
        out_shape=(
            jax.ShapeDtypeStruct((rows, width), bf16),
            jax.ShapeDtypeStruct((rows, width), f32),
            jax.ShapeDtypeStruct((cols, rows, width), bf16),
            jax.ShapeDtypeStruct((requests, cands), f32),
        ),
        in_specs=[pl.BlockSpec(memory_space=pltpu.VMEM)] * 7,
        out_specs=(pl.BlockSpec(memory_space=pltpu.VMEM),) * 4,
        scratch_shapes=[
            pltpu.VMEM((rows, width), bf16),
            pltpu.VMEM((rows // steps, requests), f32),
            pltpu.VMEM((cands, 8, requests), f32),
            pltpu.VMEM((requests, width), bf16),
            pltpu.VMEM((cands, requests), f32),
            pltpu.VMEM((cands, requests), f32),
            pltpu.VMEM((rows, requests), f32),
            pltpu.VMEM((rows, width), f32),
            pltpu.VMEM((rows // steps, width), f32),
            pltpu.VMEM((2, cols, rows, width), bf16),
            pltpu.VMEM((2, cols, rows, width), bf16),
            moves,
            moves,
            moves,
            moves,
        ],
        compiler_params=pltpu.CompilerParams(
            collective_id=2, has_side_effects=True, vmem_limit_bytes=VMEM_LIMIT
        ),
        name="node_step",
    )(items, parts, w_self, w_neighbor, bias[None], gain[None], packed)


def body(
    item_features,
    self_weight,
    neighbor_weight,
    layer_bias,
    norm_gain,
    blocks,
    block_rows,
    block_cols,
    counts,
    queries,
    candidates,
    positions,
    position_table,
    tower_weight,
    score_cotangent,
):
    rows_dev, width = item_features.shape
    tiles = blocks[0, 0]
    block = tiles.shape[1]
    cands = candidates.shape[1]
    col_count = lax.axis_size("col")
    row_count = lax.axis_size("row")
    column_items, packed = gather_rows(
        row_count, item_features, queries, candidates, score_cotangent
    )
    tower_values = jnp.sum(jax.nn.relu(position_table) * tower_weight, axis=-1)
    position_hits = positions[..., None] == jnp.arange(tower_values.shape[0])
    position_scores = jnp.sum(jnp.where(position_hits, tower_values, 0.0), axis=-1)

    (parts,) = block_products(
        tiles, block_rows[0, 0], block_cols[0, 0], counts[0],
        column_items, col_count * rows_dev // block, False,
    )
    hidden, grad_self, range_source, raw = node_step(
        col_count, item_features, parts.reshape(col_count, rows_dev, width), self_weight,
        neighbor_weight, layer_bias, norm_gain, packed.reshape(-1, packed.shape[-1]), cands,
    )
    back_parts, hidden = block_products(
        tiles, block_cols[0, 0], block_rows[0, 0], counts[0],
        range_source, row_count * rows_dev // block, True, (hidden,),
    )
    item_grads, scores = scatter_rows(
        row_count,
        back_parts.reshape(row_count, rows_dev, width),
        raw.reshape(row_count, -1, cands),
        grad_self,
        position_scores,
        width ** (-0.5),
    )
    return (hidden, scores, item_grads)


def solution(mesh):
    in_specs = (
        P(("row", "col"), None),
        P(),
        P(),
        P(),
        P(),
        P("row", "col", None, None, None),
        P("row", "col", None),
        P("row", "col", None),
        P("row", "col"),
        P(("row", "col"), None),
        P(("row", "col"), None),
        P(("row", "col"), None),
        P(),
        P(),
        P(("row", "col"), None),
    )
    out_specs = (P(("row", "col"), None), P(("row", "col"), None), P(("row", "col"), None))
    return jax.shard_map(body, mesh=mesh, in_specs=in_specs, out_specs=out_specs, check_vma=False)
```

```python
import functools

import jax
import jax.numpy as jnp
from jax import lax
from jax.experimental import pallas as pl
from jax.experimental.pallas import tpu as pltpu
from jax.sharding import PartitionSpec as P

norm_eps = 1e-05
f32 = jnp.float32
bf16 = jnp.bfloat16
VMEM_LIMIT = 56 * 1024 * 1024


def dot(a, b, dims=((1,), (0,))):
    return lax.dot_general(a, b, (dims, ((), ())), preferred_element_type=f32)


def block_kernel(
    transpose, chunk, unroll, targets, sources, count, tiles, source, *refs
):
    kept = (len(refs) - 6) // 2
    out = refs[kept]
    even, odd, held, held_source, arrived, source_arrived = refs[2 * kept + 1 :]
    totals = (even, odd)
    target_blocks = out.shape[0]
    chunks = tiles.shape[0] // chunk
    live = count[0]

    def fetch(index):
        span = pl.ds(index * chunk, chunk)
        return pltpu.make_async_copy(tiles.at[span], held.at[span], arrived.at[index])

    fetch_source = pltpu.make_async_copy(source, held_source, source_arrived)
    fetch_source.start()
    for index in range(chunks):

        @pl.when(index * chunk < live)
        def _():
            fetch(index).start()

    for total in totals:
        total[...] = jnp.zeros_like(total)
    for n in range(kept):
        refs[kept + 1 + n][...] = refs[n][...]
    fetch_source.wait()

    def group(index, carry):
        dims = ((0,), (0,)) if transpose else ((1,), (0,))
        for lane in range(unroll):
            place = index * unroll + lane
            target = jnp.where(place < live, targets[place], target_blocks)
            product = dot(held[place], held_source[sources[place]], dims)
            totals[lane % 2][target] += product
        return carry

    def part(index, carry):
        fetch(index).wait()
        start = index * (chunk // unroll)
        stop = jnp.minimum(start + chunk // unroll, (live + unroll - 1) // unroll)
        return lax.fori_loop(start, stop, group, carry)

    lax.fori_loop(0, (live + chunk - 1) // chunk, part, 0)
    out[...] = (even[0:target_blocks] + odd[0:target_blocks]).astype(out.dtype)


def block_products(tiles, targets, sources, count, source, target_blocks, transpose, kept=()):
    slots, block, _ = tiles.shape
    width = source.shape[-1]
    chunk = min(16, slots)
    shaped = source.reshape(-1, block, width)
    whole = pl.BlockSpec(memory_space=pltpu.VMEM)
    scalars = pl.BlockSpec(memory_space=pltpu.SMEM)
    stays = pl.BlockSpec(memory_space=pl.ANY)
    out, *rest = pl.pallas_call(
        functools.partial(block_kernel, transpose, chunk, min(8, chunk)),
        in_specs=[scalars] * 3 + [stays] * 2 + [whole] * len(kept),
        out_specs=(whole,) * (1 + len(kept)),
        scratch_shapes=[
            pltpu.VMEM((target_blocks + 1, block, width), f32),
            pltpu.VMEM((target_blocks + 1, block, width), f32),
            pltpu.VMEM(tiles.shape, bf16),
            pltpu.VMEM(shaped.shape, bf16),
            pltpu.SemaphoreType.DMA((slots // chunk,)),
            pltpu.SemaphoreType.DMA,
        ],
        out_shape=(jax.ShapeDtypeStruct((target_blocks, block, width), bf16),)
        + tuple(jax.ShapeDtypeStruct(array.shape, array.dtype) for array in kept),
        compiler_params=pltpu.CompilerParams(vmem_limit_bytes=VMEM_LIMIT),
        name="block_products",
    )(targets, sources, count, tiles, shaped, *kept)
    return (out.reshape(target_blocks * block, width), *rest)


def node_math(base, aggregate, w_neighbor, gain, weights, queries):
    width = base.shape[1]
    preact = base + dot(aggregate.astype(bf16), w_neighbor)
    gate = 1.0 / (1.0 + jnp.exp(-preact))
    active = preact * gate
    scale = lax.rsqrt(jnp.mean(active * active, axis=-1, keepdims=True) + norm_eps)
    hidden = (gain * active * scale).astype(bf16)
    high = weights.astype(bf16)
    low = (weights - high.astype(f32)).astype(bf16)
    grad_hidden = (dot(high, queries) + dot(low, queries)) * (width ** -0.5)
    scaled = gain * grad_hidden
    along = jnp.sum(scaled * active, axis=-1, keepdims=True) * (1.0 / width)
    grad_active = scale * scaled - active * (scale * scale * scale * along)
    grad_preact = grad_active * (gate * (1.0 + preact * (1.0 - gate)))
    return hidden, grad_preact.astype(bf16)


def remote(src, dst, send, recv, place):
    return pltpu.make_async_remote_copy(
        src_ref=src, dst_ref=dst, send_sem=send, recv_sem=recv,
        device_id=place, device_id_type=pl.DeviceIdType.MESH,
    )


def greet(places):
    barrier = pltpu.get_barrier_semaphore()
    for place in places:
        pl.semaphore_signal(
            barrier, inc=1, device_id=place, device_id_type=pl.DeviceIdType.MESH
        )
    pl.semaphore_wait(barrier, len(places))


def row_places(chips):
    me = lax.axis_index("row")
    core = lax.rem(me, 2)
    chip = me // 2
    ahead = [lax.rem(chip + i, chips) for i in range(chips)]
    behind = [lax.rem(chip + chips - i, chips) for i in range(chips)]
    return me, core, ahead, behind


def gather_kernel(
    chips, items, queries, candidates, cotangent, all_items, all_packed, packed, send, recv
):
    arrays = 2
    inputs, outputs = (items, packed), (all_items, all_packed)
    me, core, ahead, behind = row_places(chips)
    sibling = {"row": me + 1 - 2 * core}
    peers = [{"row": ahead[i] * 2 + core} for i in range(chips)]
    packed[...] = jnp.concatenate(
        [ref[...].astype(f32) for ref in (queries, candidates, cotangent)], axis=1
    )
    greet(peers[1:] + [sibling])
    copies = []
    for n in range(arrays):
        for i in range(1, chips):
            copy = remote(
                inputs[n], outputs[n].at[me], send.at[n, i], recv.at[n, i], peers[i]
            )
            copy.start()
            copies.append(copy)
    for n in range(arrays):
        copy = remote(
            inputs[n], outputs[n].at[me], send.at[n, chips], recv.at[n, chips], sibling
        )
        copy.start()
        copies.append(copy)
    own = [
        pltpu.make_async_copy(inputs[n], outputs[n].at[me], send.at[n, 0])
        for n in range(arrays)
    ]
    for copy in own:
        copy.start()
    forwards = []
    for n in reversed(range(arrays)):
        for i in range(1, chips):
            copies[n * (chips - 1) + i - 1].wait_recv()
            piece = outputs[n].at[behind[i] * 2 + core]
            copy = remote(
                piece, piece, send.at[n, chips + i], recv.at[n, chips + i], sibling
            )
            copy.start()
            forwards.append(copy)
    for copy in copies[arrays * (chips - 1) :]:
        copy.wait_recv()
    for copy in forwards:
        copy.wait_recv()
    for copy in copies + forwards:
        copy.wait_send()
    for copy in own:
        copy.wait()


def gather_rows(row_count, items, queries, candidates, cotangent):
    chips = row_count // 2
    small = (queries, candidates, cotangent)
    packed = (queries.shape[0], sum(array.shape[1] for array in small))
    return pl.pallas_call(
        functools.partial(gather_kernel, chips),
        out_shape=(
            jax.ShapeDtypeStruct((row_count,) + items.shape, items.dtype),
            jax.ShapeDtypeStruct((row_count,) + packed, f32),
        ),
        in_specs=[pl.BlockSpec(memory_space=pl.ANY)]
        + [pl.BlockSpec(memory_space=pltpu.VMEM)] * 3,
        out_specs=(pl.BlockSpec(memory_space=pl.ANY),) * 2,
        scratch_shapes=[
            pltpu.VMEM(packed, f32),
            pltpu.SemaphoreType.DMA((2, 2 * chips)),
            pltpu.SemaphoreType.DMA((2, 2 * chips)),
        ],
        compiler_params=pltpu.CompilerParams(
            collective_id=0, has_side_effects=True, vmem_limit_bytes=VMEM_LIMIT
        ),
        name="gather_rows",
    )(items, *small)


def scatter_kernel(
    chips, scale, parts, raw, grad_self, position_scores, grads, scores,
    near, sums, far, near_raw, sums_raw, far_raw, send, recv,
):
    me, core, ahead, behind = row_places(chips)
    sibling = {"row": me + 1 - 2 * core}
    peers = [{"row": ahead[i] * 2 + core} for i in range(chips)]
    greet(peers[1:] + [sibling])
    order = list(range(1, chips)) + [0]
    arrays = ((parts, near, sums, far), (raw, near_raw, sums_raw, far_raw))
    first = {}
    for i in order:
        for n, (mine, inbox, _, _) in enumerate(arrays):
            first[n, i] = remote(
                mine.at[ahead[i] * 2 + 1 - core], inbox.at[i],
                send.at[n, i], recv.at[n, i], sibling,
            )
    for i in order:
        first[1, i].start()
    first[0, order[0]].start()
    second = []
    for turn, i in enumerate(order):
        first[0, i].wait_send()
        if turn + 1 < chips:
            first[0, order[turn + 1]].start()
        for n, (mine, inbox, summed, outbox) in enumerate(arrays):
            first[n, i].wait_recv()
            value = mine[ahead[i] * 2 + core].astype(f32) + inbox[i].astype(f32)
            if i == 0:
                if n == 0:
                    grads[...] = grad_self[...] + value
                else:
                    scores[...] = value
            else:
                summed[i] = value.astype(summed.dtype)
                copy = remote(
                    summed.at[i], outbox.at[i],
                    send.at[n, chips + i], recv.at[n, chips + i], peers[i],
                )
                copy.start()
                second.append((n, i, copy))
    for n, i, copy in second:
        copy.wait_recv()
        if n == 0:
            grads[...] += far[i].astype(f32)
        else:
            scores[...] += far_raw[i]
    scores[...] = scores[...] * scale + position_scores[...]
    for i in order:
        first[1, i].wait_send()
    for _, _, copy in second:
        copy.wait_send()


def scatter_rows(row_count, parts, raw, grad_self, position_scores, scale):
    chips = row_count // 2
    part = parts.shape[1:]
    part_raw = raw.shape[1:]
    return pl.pallas_call(
        functools.partial(scatter_kernel, chips, scale),
        out_shape=(
            jax.ShapeDtypeStruct(grad_self.shape, f32),
            jax.ShapeDtypeStruct(position_scores.shape, f32),
        ),
        in_specs=[pl.BlockSpec(memory_space=pltpu.VMEM)] * 4,
        out_specs=(pl.BlockSpec(memory_space=pltpu.VMEM),) * 2,
        scratch_shapes=[pltpu.VMEM((chips,) + part, bf16)] * 3
        + [pltpu.VMEM((chips,) + part_raw, f32)] * 3
        + [
            pltpu.SemaphoreType.DMA((2, 2 * chips)),
            pltpu.SemaphoreType.DMA((2, 2 * chips)),
        ],
        compiler_params=pltpu.CompilerParams(
            collective_id=1, has_side_effects=True, vmem_limit_bytes=VMEM_LIMIT
        ),
        name="scatter_rows",
    )(parts, raw, grad_self, position_scores)


def node_kernel(
    cols, steps, items, parts, w_self, w_neighbor, bias, gain, packed,
    hidden, grad_self, source, raw,
    grads, table, picks, queries, ids, cot, weights, base, aggregate, inbox, outbox,
    send, recv, sum_send, sum_recv,
):
    me = lax.axis_index("col")
    piece = lax.axis_index("row") * cols + me
    first_item = piece * items.shape[0]
    cands = ids.shape[0]
    rows = items.shape[0] // steps
    width = items.shape[1]
    ways = (1, -1)
    is_inner = (me < cols - 1, me > 0)
    barrier = pltpu.get_barrier_semaphore()
    for way in range(2):

        @pl.when(is_inner[way])
        def _():
            pl.semaphore_signal(
                barrier, inc=1, device_id={"col": me + ways[way]},
                device_id_type=pl.DeviceIdType.MESH,
            )

    pl.semaphore_wait(
        barrier, is_inner[0].astype(jnp.int32) + is_inner[1].astype(jnp.int32)
    )

    def hop(way, far, j, piece):
        ref = source.at[piece, pl.ds(j * rows, rows)]
        return remote(
            ref, ref, send.at[way, far, j], recv.at[way, far, j], {"col": me + ways[way]}
        )

    def outgoing(way, far, j):
        return hop(way, far, j, me - ways[way] * far)

    def incoming(way, far, j):
        return hop(way, far, j, me - ways[way] * (far + 1))

    def has(way, far):
        return me >= far if way == 0 else me + far < cols

    def sum_hop(way, dest, j, ref):
        return remote(
            ref.at[pl.ds(j * rows, rows)], inbox.at[way, dest, pl.ds(j * rows, rows)],
            sum_send.at[way, dest, j], sum_recv.at[way, dest, j], {"col": me + ways[way]},
        )

    def is_before(way, dest):
        return me < dest if way == 0 else me > dest

    in_flight = 3
    turns = (cols - 1) * steps
    order = (
        [(cols - 1 - turn // steps, turn % steps) for turn in range(turns)],
        [(turn // steps, turn % steps) for turn in range(turns)],
    )

    def sum_part(way, turn):
        dest, j = order[way][turn]
        span = pl.ds(j * rows, rows)
        is_end = me == (0 if way == 0 else cols - 1)

        @pl.when(is_end)
        def _():
            if turn >= in_flight:
                old = order[way][turn - in_flight]
                sum_hop(way, *old, parts.at[old[0]]).wait_send()
            sum_hop(way, dest, j, parts.at[dest]).start()

        @pl.when(is_before(way, dest) & jnp.logical_not(is_end))
        def _():
            sum_hop(way, dest, j, parts.at[dest]).wait_recv()
            outbox[way, dest, span, :] = (
                parts[dest, span, :].astype(f32) + inbox[way, dest, span, :].astype(f32)
            ).astype(bf16)
            sum_hop(way, dest, j, outbox.at[way, dest]).start()

    for turn in range(turns):
        sum_part(0, turn)
        sum_part(1, turn)

    queries[...] = packed[:, :width].astype(bf16)
    tail = packed[:, width:].T
    ids[...] = tail[:cands]
    cot[...] = tail[cands:]
    for j in range(steps):
        span = pl.ds(j * rows, rows)
        weights[span, :] = part_weights(ids, cot, first_item + j * rows, rows)
        base[span, :] = dot(items[span, :], w_self[...]) + bias[...]

    def node_part(j):
        span = pl.ds(j * rows, rows)
        aggregate[...] = parts[me, span, :].astype(f32)
        for way in range(2):

            @pl.when(is_inner[1 - way])
            def _():
                sum_hop(way, me, j, parts.at[me]).wait_recv()
                aggregate[...] += inbox[way, me, span, :].astype(f32)

        new, grad = node_math(
            base[span, :], aggregate[...], w_neighbor[...], gain[...], weights[span, :],
            queries[...],
        )
        hidden[span, :] = new
        grads[span, :] = grad
        source[me, span, :] = dot(grad, w_neighbor[...], ((1,), (1,))).astype(bf16)
        for way in range(2):

            @pl.when(is_inner[way])
            def _():
                outgoing(way, 0, j).start()

    def late_part(j):
        span = pl.ds(j * rows, rows)
        last = ((1,), (1,))
        grad_self[span, :] = dot(grads[span, :], w_self[...], last)
        table[...] = dot(hidden[span, :], queries[...], last)
        part_scores(ids, table, first_item + j * rows, rows, picks)

    picks[...] = jnp.zeros_like(picks)
    for j in range(steps):
        node_part(j)
    for far in range(cols - 1):
        for j in range(steps):
            if far == 0:
                late_part(j)
            for way in range(2):

                @pl.when(has(way, far + 1))
                def _():
                    incoming(way, far, j).wait_recv()

                if far + 1 < cols - 1:

                    @pl.when(has(way, far + 1) & is_inner[way])
                    def _():
                        outgoing(way, far + 1, j).start()

    raw[...] = jnp.sum(picks[...], axis=1).T
    for far in range(cols - 1):
        for j in range(steps):
            for way in range(2):

                @pl.when(has(way, far) & is_inner[way])
                def _():
                    outgoing(way, far, j).wait_send()

    for turn in range(turns):
        for way in range(2):
            dest, j = order[way][turn]
            is_left = is_before(way, dest)
            if turn < turns - in_flight:
                is_left &= me != (0 if way == 0 else cols - 1)

            @pl.when(is_left)
            def _():
                sum_hop(way, dest, j, parts.at[dest]).wait_send()


def part_weights(ids, cot, start, rows):
    queries = ids.shape[1]
    numbers = (lax.broadcasted_iota(jnp.int32, (rows, queries), 0) + start).astype(f32)
    acc = jnp.zeros((rows, queries), f32)
    for k in range(ids.shape[0]):
        acc += jnp.where(numbers == ids[k : k + 1, :], cot[k : k + 1, :], 0.0)
    return acc


def part_scores(ids, table, start, rows, picks):
    queries = ids.shape[1]
    numbers = (lax.broadcasted_iota(jnp.int32, (rows, queries), 0) + start).astype(f32)
    values = table[...]
    for k in range(ids.shape[0]):
        hit = jnp.where(numbers == ids[k : k + 1, :], values, 0.0)
        picks[k] += jnp.sum(hit.reshape(rows // 8, 8, queries), axis=0)


def node_step(cols, items, parts, w_self, w_neighbor, bias, gain, packed, cands):
    rows, width = items.shape
    requests = packed.shape[0]
    steps = max(rows // 128, 1)
    moves = pltpu.SemaphoreType.DMA((2, cols, steps))
    return pl.pallas_call(
        functools.partial(node_kernel, cols, steps),
        out_shape=(
            jax.ShapeDtypeStruct((rows, width), bf16),
            jax.ShapeDtypeStruct((rows, width), f32),
            jax.ShapeDtypeStruct((cols, rows, width), bf16),
            jax.ShapeDtypeStruct((requests, cands), f32),
        ),
        in_specs=[pl.BlockSpec(memory_space=pltpu.VMEM)] * 7,
        out_specs=(pl.BlockSpec(memory_space=pltpu.VMEM),) * 4,
        scratch_shapes=[
            pltpu.VMEM((rows, width), bf16),
            pltpu.VMEM((rows // steps, requests), f32),
            pltpu.VMEM((cands, 8, requests), f32),
            pltpu.VMEM((requests, width), bf16),
            pltpu.VMEM((cands, requests), f32),
            pltpu.VMEM((cands, requests), f32),
            pltpu.VMEM((rows, requests), f32),
            pltpu.VMEM((rows, width), f32),
            pltpu.VMEM((rows // steps, width), f32),
            pltpu.VMEM((2, cols, rows, width), bf16),
            pltpu.VMEM((2, cols, rows, width), bf16),
            moves,
            moves,
            moves,
            moves,
        ],
        compiler_params=pltpu.CompilerParams(
            collective_id=2, has_side_effects=True, vmem_limit_bytes=VMEM_LIMIT
        ),
        name="node_step",
    )(items, parts, w_self, w_neighbor, bias[None], gain[None], packed)


def body(
    item_features,
    self_weight,
    neighbor_weight,
    layer_bias,
    norm_gain,
    blocks,
    block_rows,
    block_cols,
    counts,
    queries,
    candidates,
    positions,
    position_table,
    tower_weight,
    score_cotangent,
):
    rows_dev, width = item_features.shape
    tiles = blocks[0, 0]
    block = tiles.shape[1]
    cands = candidates.shape[1]
    col_count = lax.axis_size("col")
    row_count = lax.axis_size("row")
    column_items, packed = gather_rows(
        row_count, item_features, queries, candidates, score_cotangent
    )
    tower_values = jnp.sum(jax.nn.relu(position_table) * tower_weight, axis=-1)
    position_hits = positions[..., None] == jnp.arange(tower_values.shape[0])
    position_scores = jnp.sum(jnp.where(position_hits, tower_values, 0.0), axis=-1)

    (parts,) = block_products(
        tiles, block_rows[0, 0], block_cols[0, 0], counts[0],
        column_items, col_count * rows_dev // block, False,
    )
    hidden, grad_self, range_source, raw = node_step(
        col_count, item_features, parts.reshape(col_count, rows_dev, width), self_weight,
        neighbor_weight, layer_bias, norm_gain, packed.reshape(-1, packed.shape[-1]), cands,
    )
    back_parts, hidden = block_products(
        tiles, block_cols[0, 0], block_rows[0, 0], counts[0],
        range_source, row_count * rows_dev // block, True, (hidden,),
    )
    item_grads, scores = scatter_rows(
        row_count,
        back_parts.reshape(row_count, rows_dev, width),
        raw.reshape(row_count, -1, cands),
        grad_self,
        position_scores,
        width ** (-0.5),
    )
    return (hidden, scores, item_grads)


def solution(mesh):
    in_specs = (
        P(("row", "col"), None),
        P(),
        P(),
        P(),
        P(),
        P("row", "col", None, None, None),
        P("row", "col", None),
        P("row", "col", None),
        P("row", "col"),
        P(("row", "col"), None),
        P(("row", "col"), None),
        P(("row", "col"), None),
        P(),
        P(),
        P(("row", "col"), None),
    )
    out_specs = (P(("row", "col"), None), P(("row", "col"), None), P(("row", "col"), None))
    return jax.shard_map(body, mesh=mesh, in_specs=in_specs, out_specs=out_specs, check_vma=False)
```

```python
import functools

import jax
import jax.numpy as jnp
from jax import lax
from jax.experimental import pallas as pl
from jax.experimental.pallas import tpu as pltpu
from jax.sharding import PartitionSpec as P

norm_eps = 1e-05
f32 = jnp.float32
bf16 = jnp.bfloat16
VMEM_LIMIT = 56 * 1024 * 1024


def dot(a, b, dims=((1,), (0,))):
    return lax.dot_general(a, b, (dims, ((), ())), preferred_element_type=f32)


def block_kernel(
    transpose, chunk, unroll, targets, sources, count, tiles, source, *refs
):
    kept = (len(refs) - 6) // 2
    out = refs[kept]
    even, odd, held, held_source, arrived, source_arrived = refs[2 * kept + 1 :]
    totals = (even, odd)
    target_blocks = out.shape[0]
    chunks = tiles.shape[0] // chunk
    live = count[0]

    def fetch(index):
        span = pl.ds(index * chunk, chunk)
        return pltpu.make_async_copy(tiles.at[span], held.at[span], arrived.at[index])

    fetch_source = pltpu.make_async_copy(source, held_source, source_arrived)
    fetch_source.start()
    for index in range(chunks):

        @pl.when(index * chunk < live)
        def _():
            fetch(index).start()

    for total in totals:
        total[...] = jnp.zeros_like(total)
    for n in range(kept):
        refs[kept + 1 + n][...] = refs[n][...]
    fetch_source.wait()

    def group(index, carry):
        dims = ((0,), (0,)) if transpose else ((1,), (0,))
        for lane in range(unroll):
            place = index * unroll + lane
            target = jnp.where(place < live, targets[place], target_blocks)
            product = dot(held[place], held_source[sources[place]], dims)
            totals[lane % 2][target] += product
        return carry

    def part(index, carry):
        fetch(index).wait()
        start = index * (chunk // unroll)
        stop = jnp.minimum(start + chunk // unroll, (live + unroll - 1) // unroll)
        return lax.fori_loop(start, stop, group, carry)

    lax.fori_loop(0, (live + chunk - 1) // chunk, part, 0)
    out[...] = (even[0:target_blocks] + odd[0:target_blocks]).astype(out.dtype)


def block_products(tiles, targets, sources, count, source, target_blocks, transpose, kept=()):
    slots, block, _ = tiles.shape
    width = source.shape[-1]
    chunk = min(16, slots)
    shaped = source.reshape(-1, block, width)
    whole = pl.BlockSpec(memory_space=pltpu.VMEM)
    scalars = pl.BlockSpec(memory_space=pltpu.SMEM)
    stays = pl.BlockSpec(memory_space=pl.ANY)
    out, *rest = pl.pallas_call(
        functools.partial(block_kernel, transpose, chunk, min(8, chunk)),
        in_specs=[scalars] * 3 + [stays] * 2 + [whole] * len(kept),
        out_specs=(whole,) * (1 + len(kept)),
        scratch_shapes=[
            pltpu.VMEM((target_blocks + 1, block, width), f32),
            pltpu.VMEM((target_blocks + 1, block, width), f32),
            pltpu.VMEM(tiles.shape, bf16),
            pltpu.VMEM(shaped.shape, bf16),
            pltpu.SemaphoreType.DMA((slots // chunk,)),
            pltpu.SemaphoreType.DMA,
        ],
        out_shape=(jax.ShapeDtypeStruct((target_blocks, block, width), bf16),)
        + tuple(jax.ShapeDtypeStruct(array.shape, array.dtype) for array in kept),
        compiler_params=pltpu.CompilerParams(vmem_limit_bytes=VMEM_LIMIT),
        name="block_products",
    )(targets, sources, count, tiles, shaped, *kept)
    return (out.reshape(target_blocks * block, width), *rest)


def node_math(base, aggregate, w_neighbor, gain, weights, queries):
    width = base.shape[1]
    preact = base + dot(aggregate.astype(bf16), w_neighbor)
    gate = 1.0 / (1.0 + jnp.exp(-preact))
    active = preact * gate
    scale = lax.rsqrt(jnp.mean(active * active, axis=-1, keepdims=True) + norm_eps)
    hidden = (gain * active * scale).astype(bf16)
    high = weights.astype(bf16)
    low = (weights - high.astype(f32)).astype(bf16)
    grad_hidden = (dot(high, queries) + dot(low, queries)) * (width ** -0.5)
    scaled = gain * grad_hidden
    along = jnp.sum(scaled * active, axis=-1, keepdims=True) * (1.0 / width)
    grad_active = scale * scaled - active * (scale * scale * scale * along)
    grad_preact = grad_active * (gate * (1.0 + preact * (1.0 - gate)))
    return hidden, grad_preact.astype(bf16)


def remote(src, dst, send, recv, place):
    return pltpu.make_async_remote_copy(
        src_ref=src, dst_ref=dst, send_sem=send, recv_sem=recv,
        device_id=place, device_id_type=pl.DeviceIdType.MESH,
    )


def greet(places):
    barrier = pltpu.get_barrier_semaphore()
    for place in places:
        pl.semaphore_signal(
            barrier, inc=1, device_id=place, device_id_type=pl.DeviceIdType.MESH
        )
    pl.semaphore_wait(barrier, len(places))


def row_places(chips):
    me = lax.axis_index("row")
    core = lax.rem(me, 2)
    chip = me // 2
    ahead = [lax.rem(chip + i, chips) for i in range(chips)]
    behind = [lax.rem(chip + chips - i, chips) for i in range(chips)]
    return me, core, ahead, behind


def gather_kernel(
    chips, items, queries, candidates, cotangent, all_items, all_packed, packed, send, recv
):
    arrays = 2
    inputs, outputs = (items, packed), (all_items, all_packed)
    me, core, ahead, behind = row_places(chips)
    sibling = {"row": me + 1 - 2 * core}
    peers = [{"row": ahead[i] * 2 + core} for i in range(chips)]
    packed[...] = jnp.concatenate(
        [ref[...].astype(f32) for ref in (queries, candidates, cotangent)], axis=1
    )
    greet(peers[1:] + [sibling])
    copies = []
    for n in range(arrays):
        for i in range(1, chips):
            copy = remote(
                inputs[n], outputs[n].at[me], send.at[n, i], recv.at[n, i], peers[i]
            )
            copy.start()
            copies.append(copy)
    for n in range(arrays):
        copy = remote(
            inputs[n], outputs[n].at[me], send.at[n, chips], recv.at[n, chips], sibling
        )
        copy.start()
        copies.append(copy)
    own = [
        pltpu.make_async_copy(inputs[n], outputs[n].at[me], send.at[n, 0])
        for n in range(arrays)
    ]
    for copy in own:
        copy.start()
    forwards = []
    for n in reversed(range(arrays)):
        for i in range(1, chips):
            copies[n * (chips - 1) + i - 1].wait_recv()
            piece = outputs[n].at[behind[i] * 2 + core]
            copy = remote(
                piece, piece, send.at[n, chips + i], recv.at[n, chips + i], sibling
            )
            copy.start()
            forwards.append(copy)
    for copy in copies[arrays * (chips - 1) :]:
        copy.wait_recv()
    for copy in forwards:
        copy.wait_recv()
    for copy in copies + forwards:
        copy.wait_send()
    for copy in own:
        copy.wait()


def gather_rows(row_count, items, queries, candidates, cotangent):
    chips = row_count // 2
    small = (queries, candidates, cotangent)
    packed = (queries.shape[0], sum(array.shape[1] for array in small))
    return pl.pallas_call(
        functools.partial(gather_kernel, chips),
        out_shape=(
            jax.ShapeDtypeStruct((row_count,) + items.shape, items.dtype),
            jax.ShapeDtypeStruct((row_count,) + packed, f32),
        ),
        in_specs=[pl.BlockSpec(memory_space=pl.ANY)]
        + [pl.BlockSpec(memory_space=pltpu.VMEM)] * 3,
        out_specs=(pl.BlockSpec(memory_space=pl.ANY),) * 2,
        scratch_shapes=[
            pltpu.VMEM(packed, f32),
            pltpu.SemaphoreType.DMA((2, 2 * chips)),
            pltpu.SemaphoreType.DMA((2, 2 * chips)),
        ],
        compiler_params=pltpu.CompilerParams(
            collective_id=0, has_side_effects=True, vmem_limit_bytes=VMEM_LIMIT
        ),
        name="gather_rows",
    )(items, *small)


def scatter_kernel(
    chips, scale, parts, raw, grad_self, positions, table, tower, grads, scores,
    near, sums, far, near_raw, sums_raw, far_raw, send, recv,
):
    me, core, ahead, behind = row_places(chips)
    sibling = {"row": me + 1 - 2 * core}
    peers = [{"row": ahead[i] * 2 + core} for i in range(chips)]
    greet(peers[1:] + [sibling])
    order = list(range(1, chips)) + [0]
    arrays = ((parts, near, sums, far), (raw, near_raw, sums_raw, far_raw))
    first = {}
    for i in order:
        for n, (mine, inbox, _, _) in enumerate(arrays):
            first[n, i] = remote(
                mine.at[ahead[i] * 2 + 1 - core], inbox.at[i],
                send.at[n, i], recv.at[n, i], sibling,
            )
            first[n, i].start()
    second = []
    for i in order:
        for n, (mine, inbox, summed, outbox) in enumerate(arrays):
            first[n, i].wait_recv()
            value = mine[ahead[i] * 2 + core].astype(f32) + inbox[i].astype(f32)
            if i == 0:
                if n == 0:
                    grads[...] = grad_self[...] + value
                else:
                    scores[...] = value
            else:
                summed[i] = value.astype(summed.dtype)
                copy = remote(
                    summed.at[i], outbox.at[i],
                    send.at[n, chips + i], recv.at[n, chips + i], peers[i],
                )
                copy.start()
                second.append((n, i, copy))
    tower_values = jnp.sum(
        jnp.maximum(table[...], 0.0) * tower[...], axis=-1, keepdims=True
    )
    places = positions[...]
    position_scores = jnp.zeros(places.shape, f32)
    for place in range(tower_values.shape[0]):
        position_scores += jnp.where(
            places == place, tower_values[place : place + 1, :], 0.0
        )
    for n, i, copy in second:
        copy.wait_recv()
        if n == 0:
            grads[...] += far[i].astype(f32)
        else:
            scores[...] += far_raw[i]
    scores[...] = scores[...] * scale + position_scores
    for copy in first.values():
        copy.wait_send()
    for _, _, copy in second:
        copy.wait_send()


def scatter_rows(row_count, parts, raw, grad_self, positions, table, tower, scale):
    chips = row_count // 2
    part = parts.shape[1:]
    part_raw = raw.shape[1:]
    return pl.pallas_call(
        functools.partial(scatter_kernel, chips, scale),
        out_shape=(
            jax.ShapeDtypeStruct(grad_self.shape, f32),
            jax.ShapeDtypeStruct(positions.shape, f32),
        ),
        in_specs=[pl.BlockSpec(memory_space=pltpu.VMEM)] * 6,
        out_specs=(pl.BlockSpec(memory_space=pltpu.VMEM),) * 2,
        scratch_shapes=[pltpu.VMEM((chips,) + part, bf16)] * 3
        + [pltpu.VMEM((chips,) + part_raw, f32)] * 3
        + [
            pltpu.SemaphoreType.DMA((2, 2 * chips)),
            pltpu.SemaphoreType.DMA((2, 2 * chips)),
        ],
        compiler_params=pltpu.CompilerParams(
            collective_id=1, has_side_effects=True, vmem_limit_bytes=VMEM_LIMIT
        ),
        name="scatter_rows",
    )(parts, raw, grad_self, positions, table, tower[None])


def node_kernel(
    cols, steps, items, parts, w_self, w_neighbor, bias, gain, packed,
    hidden, grad_self, source, raw,
    grads, table, picks, queries, ids, cot, weights, base, aggregate, inbox, outbox,
    send, recv, sum_send, sum_recv,
):
    me = lax.axis_index("col")
    piece = lax.axis_index("row") * cols + me
    first_item = piece * items.shape[0]
    cands = ids.shape[0]
    rows = items.shape[0] // steps
    width = items.shape[1]
    ways = (1, -1)
    is_inner = (me < cols - 1, me > 0)
    barrier = pltpu.get_barrier_semaphore()
    for way in range(2):

        @pl.when(is_inner[way])
        def _():
            pl.semaphore_signal(
                barrier, inc=1, device_id={"col": me + ways[way]},
                device_id_type=pl.DeviceIdType.MESH,
            )

    pl.semaphore_wait(
        barrier, is_inner[0].astype(jnp.int32) + is_inner[1].astype(jnp.int32)
    )

    def hop(way, far, j, piece):
        ref = source.at[piece, pl.ds(j * rows, rows)]
        return remote(
            ref, ref, send.at[way, far, j], recv.at[way, far, j], {"col": me + ways[way]}
        )

    def outgoing(way, far, j):
        return hop(way, far, j, me - ways[way] * far)

    def incoming(way, far, j):
        return hop(way, far, j, me - ways[way] * (far + 1))

    def has(way, far):
        return me >= far if way == 0 else me + far < cols

    def sum_hop(way, dest, j, ref):
        return remote(
            ref.at[pl.ds(j * rows, rows)], inbox.at[way, dest, pl.ds(j * rows, rows)],
            sum_send.at[way, dest, j], sum_recv.at[way, dest, j], {"col": me + ways[way]},
        )

    def is_before(way, dest):
        return me < dest if way == 0 else me > dest

    in_flight = 3
    turns = (cols - 1) * steps
    order = (
        [(cols - 1 - turn // steps, turn % steps) for turn in range(turns)],
        [(turn // steps, turn % steps) for turn in range(turns)],
    )

    def sum_part(way, turn):
        dest, j = order[way][turn]
        span = pl.ds(j * rows, rows)
        is_end = me == (0 if way == 0 else cols - 1)

        @pl.when(is_end)
        def _():
            if turn >= in_flight:
                old = order[way][turn - in_flight]
                sum_hop(way, *old, parts.at[old[0]]).wait_send()
            sum_hop(way, dest, j, parts.at[dest]).start()

        @pl.when(is_before(way, dest) & jnp.logical_not(is_end))
        def _():
            sum_hop(way, dest, j, parts.at[dest]).wait_recv()
            outbox[way, dest, span, :] = (
                parts[dest, span, :].astype(f32) + inbox[way, dest, span, :].astype(f32)
            ).astype(bf16)
            sum_hop(way, dest, j, outbox.at[way, dest]).start()

    for turn in range(turns):
        sum_part(0, turn)
        sum_part(1, turn)

    queries[...] = packed[:, :width].astype(bf16)
    tail = packed[:, width:].T
    ids[...] = tail[:cands]
    cot[...] = tail[cands:]
    for j in range(steps):
        span = pl.ds(j * rows, rows)
        weights[span, :] = part_weights(ids, cot, first_item + j * rows, rows)
        base[span, :] = dot(items[span, :], w_self[...]) + bias[...]

    def node_part(j):
        span = pl.ds(j * rows, rows)
        aggregate[...] = parts[me, span, :].astype(f32)
        for way in range(2):

            @pl.when(is_inner[1 - way])
            def _():
                sum_hop(way, me, j, parts.at[me]).wait_recv()
                aggregate[...] += inbox[way, me, span, :].astype(f32)

        new, grad = node_math(
            base[span, :], aggregate[...], w_neighbor[...], gain[...], weights[span, :],
            queries[...],
        )
        hidden[span, :] = new
        grads[span, :] = grad
        source[me, span, :] = dot(grad, w_neighbor[...], ((1,), (1,))).astype(bf16)
        for way in range(2):

            @pl.when(is_inner[way])
            def _():
                outgoing(way, 0, j).start()

    def late_part(j):
        span = pl.ds(j * rows, rows)
        last = ((1,), (1,))
        grad_self[span, :] = dot(grads[span, :], w_self[...], last)
        table[...] = dot(hidden[span, :], queries[...], last)
        part_scores(ids, table, first_item + j * rows, rows, picks)

    picks[...] = jnp.zeros_like(picks)
    for j in range(steps):
        node_part(j)
    for far in range(cols - 1):
        for j in range(steps):
            if far == 0:
                late_part(j)
            for way in range(2):

                @pl.when(has(way, far + 1))
                def _():
                    incoming(way, far, j).wait_recv()

                if far + 1 < cols - 1:

                    @pl.when(has(way, far + 1) & is_inner[way])
                    def _():
                        outgoing(way, far + 1, j).start()

    raw[...] = jnp.sum(picks[...], axis=1).T
    for far in range(cols - 1):
        for j in range(steps):
            for way in range(2):

                @pl.when(has(way, far) & is_inner[way])
                def _():
                    outgoing(way, far, j).wait_send()

    for turn in range(turns):
        for way in range(2):
            dest, j = order[way][turn]
            is_left = is_before(way, dest)
            if turn < turns - in_flight:
                is_left &= me != (0 if way == 0 else cols - 1)

            @pl.when(is_left)
            def _():
                sum_hop(way, dest, j, parts.at[dest]).wait_send()


def part_weights(ids, cot, start, rows):
    queries = ids.shape[1]
    numbers = (lax.broadcasted_iota(jnp.int32, (rows, queries), 0) + start).astype(f32)
    acc = jnp.zeros((rows, queries), f32)
    for k in range(ids.shape[0]):
        acc += jnp.where(numbers == ids[k : k + 1, :], cot[k : k + 1, :], 0.0)
    return acc


def part_scores(ids, table, start, rows, picks):
    queries = ids.shape[1]
    numbers = (lax.broadcasted_iota(jnp.int32, (rows, queries), 0) + start).astype(f32)
    values = table[...]
    for k in range(ids.shape[0]):
        hit = jnp.where(numbers == ids[k : k + 1, :], values, 0.0)
        picks[k] += jnp.sum(hit.reshape(rows // 8, 8, queries), axis=0)


def node_step(cols, items, parts, w_self, w_neighbor, bias, gain, packed, cands):
    rows, width = items.shape
    requests = packed.shape[0]
    steps = max(rows // 128, 1)
    moves = pltpu.SemaphoreType.DMA((2, cols, steps))
    return pl.pallas_call(
        functools.partial(node_kernel, cols, steps),
        out_shape=(
            jax.ShapeDtypeStruct((rows, width), bf16),
            jax.ShapeDtypeStruct((rows, width), f32),
            jax.ShapeDtypeStruct((cols, rows, width), bf16),
            jax.ShapeDtypeStruct((requests, cands), f32),
        ),
        in_specs=[pl.BlockSpec(memory_space=pltpu.VMEM)] * 7,
        out_specs=(pl.BlockSpec(memory_space=pltpu.VMEM),) * 4,
        scratch_shapes=[
            pltpu.VMEM((rows, width), bf16),
            pltpu.VMEM((rows // steps, requests), f32),
            pltpu.VMEM((cands, 8, requests), f32),
            pltpu.VMEM((requests, width), bf16),
            pltpu.VMEM((cands, requests), f32),
            pltpu.VMEM((cands, requests), f32),
            pltpu.VMEM((rows, requests), f32),
            pltpu.VMEM((rows, width), f32),
            pltpu.VMEM((rows // steps, width), f32),
            pltpu.VMEM((2, cols, rows, width), bf16),
            pltpu.VMEM((2, cols, rows, width), bf16),
            moves,
            moves,
            moves,
            moves,
        ],
        compiler_params=pltpu.CompilerParams(
            collective_id=2, has_side_effects=True, vmem_limit_bytes=VMEM_LIMIT
        ),
        name="node_step",
    )(items, parts, w_self, w_neighbor, bias[None], gain[None], packed)


def body(
    item_features,
    self_weight,
    neighbor_weight,
    layer_bias,
    norm_gain,
    blocks,
    block_rows,
    block_cols,
    counts,
    queries,
    candidates,
    positions,
    position_table,
    tower_weight,
    score_cotangent,
):
    rows_dev, width = item_features.shape
    tiles = blocks[0, 0]
    block = tiles.shape[1]
    cands = candidates.shape[1]
    col_count = lax.axis_size("col")
    row_count = lax.axis_size("row")
    column_items, packed = gather_rows(
        row_count, item_features, queries, candidates, score_cotangent
    )
    (parts,) = block_products(
        tiles, block_rows[0, 0], block_cols[0, 0], counts[0],
        column_items, col_count * rows_dev // block, False,
    )
    hidden, grad_self, range_source, raw = node_step(
        col_count, item_features, parts.reshape(col_count, rows_dev, width), self_weight,
        neighbor_weight, layer_bias, norm_gain, packed.reshape(-1, packed.shape[-1]), cands,
    )
    back_parts, hidden = block_products(
        tiles, block_cols[0, 0], block_rows[0, 0], counts[0],
        range_source, row_count * rows_dev // block, True, (hidden,),
    )
    item_grads, scores = scatter_rows(
        row_count,
        back_parts.reshape(row_count, rows_dev, width),
        raw.reshape(row_count, -1, cands),
        grad_self,
        positions,
        position_table,
        tower_weight,
        width ** (-0.5),
    )
    return (hidden, scores, item_grads)


def solution(mesh):
    in_specs = (
        P(("row", "col"), None),
        P(),
        P(),
        P(),
        P(),
        P("row", "col", None, None, None),
        P("row", "col", None),
        P("row", "col", None),
        P("row", "col"),
        P(("row", "col"), None),
        P(("row", "col"), None),
        P(("row", "col"), None),
        P(),
        P(),
        P(("row", "col"), None),
    )
    out_specs = (P(("row", "col"), None), P(("row", "col"), None), P(("row", "col"), None))
    return jax.shard_map(body, mesh=mesh, in_specs=in_specs, out_specs=out_specs, check_vma=False)
```
